32 devices in a mesh: ctx: 16 (over z, x, core), fsdp: 2 (over y).
Axes of the slice: x: 2, y: 2, z: 4, core: 2. Of those that a mesh axis runs over, the one named last changes fastest.
Arguments:
- layer_input: bfloat16 [2, 2048, 896], P('fsdp', 'ctx'), may hold values from -6 to 6
- positions: int32 [2, 2048], P('fsdp', 'ctx'), may hold values from 0 to 2047, as said below
- out_grad: bfloat16 [2, 2048, 896], P('fsdp', 'ctx'), may hold values from -6 to 6
- norm_gain: float32 [896], P(('ctx', 'fsdp')), may hold values from 0.1 to 1.9
- query_proj: float32 [896, 896], P(('ctx', 'fsdp')), may hold values from -0.1875 to 0.1875
- query_bias: float32 [896], P(('ctx', 'fsdp')), may hold values from -3 to 3
- keyval_proj: float32 [896, 256], P(('ctx', 'fsdp')), may hold values from -0.1875 to 0.1875
- value_bias: float32 [128], P(('ctx', 'fsdp')), may hold values from -0.3 to 0.3
- output_proj: float32 [896, 896], P(('ctx', 'fsdp')), may hold values from -8 to 8
- mlp_gain: float32 [896], P(('ctx', 'fsdp')), may hold values from 0.1 to 1.9
- gate_proj: float32 [896, 4864], P(('ctx', 'fsdp')), may hold values from -0.1875 to 0.1875
- up_proj: float32 [896, 4864], P(('ctx', 'fsdp')), may hold values from -0.1875 to 0.1875
- down_proj: float32 [4864, 896], P(('ctx', 'fsdp')), may hold values from -0.078125 to 0.078125
- norm_gain_mean: float32 [896], P(('ctx', 'fsdp')), may hold values from -387.136 to 387.136
- query_proj_mean: float32 [896, 896], P(('ctx', 'fsdp')), may hold values from -223.51308 to 223.51308
- query_bias_mean: float32 [896], P(('ctx', 'fsdp')), may hold values from -223.51308 to 223.51308
- keyval_proj_mean: float32 [896, 256], P(('ctx', 'fsdp')), may hold values from -591.36 to 591.36
- value_bias_mean: float32 [128], P(('ctx', 'fsdp')), may hold values from -5352.38 to 5352.38
- output_proj_mean: float32 [896, 896], P(('ctx', 'fsdp')), may hold values from -5.5314145 to 5.5314145
- mlp_gain_mean: float32 [896], P(('ctx', 'fsdp')), may hold values from -35.84 to 35.84
- gate_proj_mean: float32 [896, 4864], P(('ctx', 'fsdp')), may hold values from -10.983624 to 10.983624
- up_proj_mean: float32 [896, 4864], P(('ctx', 'fsdp')), may hold values from -10.983624 to 10.983624
- down_proj_mean: float32 [4864, 896], P(('ctx', 'fsdp')), may hold values from -25.6 to 25.6
- norm_gain_square: float32 [896], P(('ctx', 'fsdp')), may hold values from 18235.393 to 72253.44
- query_proj_square: float32 [896, 896], P(('ctx', 'fsdp')), may hold values from 6092.8 to 24012.8
- query_bias_square: float32 [896], P(('ctx', 'fsdp')), may hold values from 6092.8 to 24012.8
- keyval_proj_square: float32 [896, 256], P(('ctx', 'fsdp')), may hold values from 42649.6 to 168089.6
- value_bias_square: float32 [128], P(('ctx', 'fsdp')), may hold values from 3493855.2 to 13872660
- output_proj_square: float32 [896, 896], P(('ctx', 'fsdp')), may hold values from 3.72272 to 14.7504
- mlp_gain_square: float32 [896], P(('ctx', 'fsdp')), may hold values from 155.648 to 614.4
- gate_proj_square: float32 [896, 4864], P(('ctx', 'fsdp')), may hold values from 14.326 to 57.304
- up_proj_square: float32 [896, 4864], P(('ctx', 'fsdp')), may hold values from 14.326 to 57.304
- down_proj_square: float32 [4864, 896], P(('ctx', 'fsdp')), may hold values from 77.824 to 311.296
Outputs:
- layer_output: bfloat16 [2, 2048, 896], P('fsdp', 'ctx')
- input_grad: float32 [2, 2048, 896], P('fsdp', 'ctx')
- grad_norm_gain: float32 [896], P(('ctx', 'fsdp'))
- grad_query_proj: float32 [896, 896], P(('ctx', 'fsdp'))
- grad_query_bias: float32 [896], P(('ctx', 'fsdp'))
- grad_keyval_proj: float32 [896, 256], P(('ctx', 'fsdp'))
- grad_value_bias: float32 [128], P(('ctx', 'fsdp'))
- grad_output_proj: float32 [896, 896], P(('ctx', 'fsdp'))
- grad_mlp_gain: float32 [896], P(('ctx', 'fsdp'))
- grad_gate_proj: float32 [896, 4864], P(('ctx', 'fsdp'))
- grad_up_proj: float32 [896, 4864], P(('ctx', 'fsdp'))
- grad_down_proj: float32 [4864, 896], P(('ctx', 'fsdp'))
- new_norm_gain: float32 [896], P(('ctx', 'fsdp'))
- new_query_proj: float32 [896, 896], P(('ctx', 'fsdp'))
- new_query_bias: float32 [896], P(('ctx', 'fsdp'))
- new_keyval_proj: float32 [896, 256], P(('ctx', 'fsdp'))
- new_value_bias: float32 [128], P(('ctx', 'fsdp'))
- new_output_proj: float32 [896, 896], P(('ctx', 'fsdp'))
- new_mlp_gain: float32 [896], P(('ctx', 'fsdp'))
- new_gate_proj: float32 [896, 4864], P(('ctx', 'fsdp'))
- new_up_proj: float32 [896, 4864], P(('ctx', 'fsdp'))
- new_down_proj: float32 [4864, 896], P(('ctx', 'fsdp'))
- new_norm_gain_mean: float32 [896], P(('ctx', 'fsdp'))
- new_query_proj_mean: float32 [896, 896], P(('ctx', 'fsdp'))
- new_query_bias_mean: float32 [896], P(('ctx', 'fsdp'))
- new_keyval_proj_mean: float32 [896, 256], P(('ctx', 'fsdp'))
- new_value_bias_mean: float32 [128], P(('ctx', 'fsdp'))
- new_output_proj_mean: float32 [896, 896], P(('ctx', 'fsdp'))
- new_mlp_gain_mean: float32 [896], P(('ctx', 'fsdp'))
- new_gate_proj_mean: float32 [896, 4864], P(('ctx', 'fsdp'))
- new_up_proj_mean: float32 [896, 4864], P(('ctx', 'fsdp'))
- new_down_proj_mean: float32 [4864, 896], P(('ctx', 'fsdp'))
- new_norm_gain_square: float32 [896], P(('ctx', 'fsdp'))
- new_query_proj_square: float32 [896, 896], P(('ctx', 'fsdp'))
- new_query_bias_square: float32 [896], P(('ctx', 'fsdp'))
- new_keyval_proj_square: float32 [896, 256], P(('ctx', 'fsdp'))
- new_value_bias_square: float32 [128], P(('ctx', 'fsdp'))
- new_output_proj_square: float32 [896, 896], P(('ctx', 'fsdp'))
- new_mlp_gain_square: float32 [896], P(('ctx', 'fsdp'))
- new_gate_proj_square: float32 [896, 4864], P(('ctx', 'fsdp'))
- new_up_proj_square: float32 [896, 4864], P(('ctx', 'fsdp'))
- new_down_proj_square: float32 [4864, 896], P(('ctx', 'fsdp'))
The draws below stay inside these ranges and needn't reach their ends.
Inputs may be any that keep to these rules, and one draw needn't show every extreme that they name: For each sequence every position appears once; the 128 rows that one index of ctx holds are block b and then block 31 - b, each of 64 consecutive positions in order, with b different on every device of the sequence.
All inputs are finite; a program needn't handle non-finite values.
Results may differ from the reference program's by a relative error of at most 0.011.
The reference program's roundings to bfloat16 on the way count: a program that leaves them out, or rounds other values in their place, can miss the bound.
Values may be sent and summed in bfloat16 or wider, within the bound.
No kernel may reach another device: no remote copies, remote signals or barrier semaphores. Data moves between devices by JAX's collectives and lax.ppermute only.
A program may use at most 320 MiB of HBM per device.

```python
import math
import jax
import jax.numpy as jnp
from jax import lax

D = 896
HEAD_DIM = 64
HEADS = 14
KV_HEADS = 2
FF = 4864
TOK_DEV = 128
ADAM_STEP = 4
GROUP = 7
SEQS = 2
SEQLEN = 2048


def draw_positions(key, part):
    device_count = SEQLEN // TOK_DEV
    half_block = TOK_DEV // 2

    def one_sequence(sequence_key):
        order = jax.random.permutation(sequence_key, device_count)
        offsets = jnp.arange(half_block, dtype=jnp.int32)
        low_block = order[:, None] * half_block + offsets[None, :]
        high_block = (2 * device_count - 1 - order)[:, None] * half_block + offsets[None, :]
        return jnp.concatenate([low_block, high_block], 1).reshape(SEQLEN)
    sequence_keys = jax.random.split(jax.random.fold_in(key, 7), SEQS)
    return jax.vmap(one_sequence)(sequence_keys).astype(jnp.int32)


def shard_levels(stream_key, dims, cuts, low, top_value):
    loudness, own = 1.0, jax.random.fold_in(stream_key, 6)
    for position, blocks in cuts:
        steps = jnp.exp(jax.random.uniform(jax.random.fold_in(own, position), (blocks,), jnp.float32, low / len(cuts), top_value / len(cuts)))
        loudness = loudness * jnp.repeat(steps, dims[position] // blocks).reshape([-1 if axis == position else 1 for axis in range(len(dims))])
    return loudness


def normal_values(stream_key, dims, width, most, cuts=(), kind=jnp.bfloat16):
    values = jax.random.normal(stream_key, dims, jnp.float32) * width
    if len(cuts) > 0:
        values = shard_levels(stream_key, dims, cuts, -0.22, 0.18) * values
    return jnp.clip(values, min=-most, max=most).astype(kind)


def setup_inputs(seed: int = 0) -> dict:
    splits = jax.random.split(jax.random.key(seed), 34)
    layer_input = normal_values(splits[0], (SEQS, SEQLEN, D), 1.0, 6.0, ((0, 2), (1, 16)))
    positions = draw_positions(jax.random.fold_in(splits[33], 71), 0)
    out_grad = normal_values(splits[2], (SEQS, SEQLEN, D), 1.0, 6.0, ((0, 2), (1, 16)))
    norm_gain = jnp.clip(1.0 + 0.18 * jax.random.normal(splits[3], (D,), jnp.float32), 0.1, 1.9)
    query_proj = normal_values(splits[4], (D, HEADS * HEAD_DIM), D ** -0.5, 0.1875, ((0, 32),), jnp.float32)
    query_bias = normal_values(splits[5], (HEADS * HEAD_DIM,), 0.5, 3.0, ((0, 32),), jnp.float32)
    keyval_proj = normal_values(splits[6], (D, 2 * KV_HEADS * HEAD_DIM), D ** -0.5, 0.1875, ((0, 32),), jnp.float32)
    value_bias = normal_values(splits[7], (KV_HEADS * HEAD_DIM,), 0.05, 0.3, ((0, 32),), jnp.float32)
    output_proj = normal_values(splits[8], (HEADS * HEAD_DIM, D), 1.5, 8.0, ((0, 32),), jnp.float32)
    mlp_gain = jnp.clip(1.0 + 0.18 * jax.random.normal(splits[9], (D,), jnp.float32), 0.1, 1.9)
    gate_proj = normal_values(splits[10], (D, FF), D ** -0.5, 0.1875, ((0, 32),), jnp.float32)
    up_proj = normal_values(splits[11], (D, FF), D ** -0.5, 0.1875, ((0, 32),), jnp.float32)
    down_proj = normal_values(splits[12], (FF, D), FF ** -0.5, 0.078125, ((0, 32),), jnp.float32)
    norm_gain_mean = normal_values(splits[13], (D,), (0.11 * (192 * SEQS * HEADS * HEAD_DIM) ** 0.5), 387.136, ((0, 32),), jnp.float32)
    query_proj_mean = normal_values(splits[14], (D, HEADS * HEAD_DIM), (0.88 * (D * SEQS) ** 0.5), 223.51308, ((0, 32),), jnp.float32)
    query_bias_mean = normal_values(splits[15], (HEADS * HEAD_DIM,), (0.88 * (D * SEQS) ** 0.5), 223.51308, ((0, 32),), jnp.float32)
    keyval_proj_mean = normal_values(splits[16], (D, 2 * KV_HEADS * HEAD_DIM), (0.88 * (D * SEQS * GROUP) ** 0.5), 591.36, ((0, 32),), jnp.float32)
    value_bias_mean = normal_values(splits[17], (KV_HEADS * HEAD_DIM,), (0.176 * (D * SEQS * SEQLEN * GROUP) ** 0.5), 5352.38, ((0, 32),), jnp.float32)
    output_proj_mean = normal_values(splits[18], (HEADS * HEAD_DIM, D), (0.11 * (SEQS * (0.0025 * SEQLEN + 30)) ** 0.5), 5.5314145, ((0, 32),), jnp.float32)
    mlp_gain_mean = normal_values(splits[19], (D,), (0.0935 * (SEQS * SEQLEN) ** 0.5), 35.84, ((0, 32),), jnp.float32)
    gate_proj_mean = normal_values(splits[20], (D, FF), (0.066 * (SEQS * SEQLEN * D // FF) ** 0.5), 10.983624, ((0, 32),), jnp.float32)
    up_proj_mean = normal_values(splits[21], (D, FF), (0.066 * (SEQS * SEQLEN * D // FF) ** 0.5), 10.983624, ((0, 32),), jnp.float32)
    down_proj_mean = normal_values(splits[22], (FF, D), (0.066 * (SEQS * SEQLEN) ** 0.5), 25.6, ((0, 32),), jnp.float32)
    norm_gain_square = jnp.clip(jnp.exp(math.log(72253.44) - 1.3768156 * jax.random.uniform(splits[23], (D,), jnp.float32) ** shard_levels(splits[23], (D,), ((0, 32),), -0.2, 0.2)), 18235.393, 72253.44)
    query_proj_square = jnp.clip(jnp.exp(math.log(24012.8) - 1.37147934 * jax.random.uniform(splits[24], (D, HEADS * HEAD_DIM), jnp.float32) ** shard_levels(splits[24], (D, HEADS * HEAD_DIM), ((0, 32),), -0.2, 0.2)), 6092.8, 24012.8)
    query_bias_square = jnp.clip(jnp.exp(math.log(24012.8) - 1.37147934 * jax.random.uniform(splits[25], (HEADS * HEAD_DIM,), jnp.float32) ** shard_levels(splits[25], (HEADS * HEAD_DIM,), ((0, 32),), -0.2, 0.2)), 6092.8, 24012.8)
    keyval_proj_square = jnp.clip(jnp.exp(math.log(168089.6) - 1.3714792 * jax.random.uniform(splits[26], (D, 2 * KV_HEADS * HEAD_DIM), jnp.float32) ** shard_levels(splits[26], (D, 2 * KV_HEADS * HEAD_DIM), ((0, 32),), -0.2, 0.2)), 42649.6, 168089.6)
    value_bias_square = jnp.clip(jnp.exp(math.log(13872660) - 1.3789142 * jax.random.uniform(splits[27], (KV_HEADS * HEAD_DIM,), jnp.float32) ** shard_levels(splits[27], (KV_HEADS * HEAD_DIM,), ((0, 32),), -0.2, 0.2)), 3493855.2, 13872660)
    output_proj_square = jnp.clip(jnp.exp(math.log(14.7504) - 1.3768156 * jax.random.uniform(splits[28], (HEADS * HEAD_DIM, D), jnp.float32) ** shard_levels(splits[28], (HEADS * HEAD_DIM, D), ((0, 32),), -0.2, 0.2)), 3.72272, 14.7504)
    mlp_gain_square = jnp.clip(jnp.exp(math.log(614.4) - 1.3730492 * jax.random.uniform(splits[29], (D,), jnp.float32) ** shard_levels(splits[29], (D,), ((0, 32),), -0.2, 0.2)), 155.648, 614.4)
    gate_proj_square = jnp.clip(jnp.exp(math.log(57.304) - 1.3862944 * jax.random.uniform(splits[30], (D, FF), jnp.float32) ** shard_levels(splits[30], (D, FF), ((0, 32),), -0.2, 0.2)), 14.326, 57.304)
    up_proj_square = jnp.clip(jnp.exp(math.log(57.304) - 1.3862944 * jax.random.uniform(splits[31], (D, FF), jnp.float32) ** shard_levels(splits[31], (D, FF), ((0, 32),), -0.2, 0.2)), 14.326, 57.304)
    down_proj_square = jnp.clip(jnp.exp(math.log(311.296) - 1.3862944 * jax.random.uniform(splits[32], (FF, D), jnp.float32) ** shard_levels(splits[32], (FF, D), ((0, 32),), -0.2, 0.2)), 77.824, 311.296)
    return {"layer_input": layer_input, "positions": positions, "out_grad": out_grad, "norm_gain": norm_gain, "query_proj": query_proj, "query_bias": query_bias, "keyval_proj": keyval_proj, "value_bias": value_bias, "output_proj": output_proj, "mlp_gain": mlp_gain, "gate_proj": gate_proj, "up_proj": up_proj, "down_proj": down_proj, "norm_gain_mean": norm_gain_mean, "query_proj_mean": query_proj_mean, "query_bias_mean": query_bias_mean, "keyval_proj_mean": keyval_proj_mean, "value_bias_mean": value_bias_mean, "output_proj_mean": output_proj_mean, "mlp_gain_mean": mlp_gain_mean, "gate_proj_mean": gate_proj_mean, "up_proj_mean": up_proj_mean, "down_proj_mean": down_proj_mean, "norm_gain_square": norm_gain_square, "query_proj_square": query_proj_square, "query_bias_square": query_bias_square, "keyval_proj_square": keyval_proj_square, "value_bias_square": value_bias_square, "output_proj_square": output_proj_square, "mlp_gain_square": mlp_gain_square, "gate_proj_square": gate_proj_square, "up_proj_square": up_proj_square, "down_proj_square": down_proj_square}


norm_eps = 1e-06
rope_base = 1000000.0
beta_first = 0.9
beta_second = 0.95
adam_eps = 1e-08
matrix_rate = 0.03
output_rate = 0.6
vector_rate = 0.5
decay_rate = 0.1
masked_score = -1e+30

def rotary_tables(position_rows, head_size):
    half_size = head_size // 2
    exponents = jnp.arange(half_size, dtype=jnp.float32) * (-2.0 / head_size)
    inverse_freq = jnp.power(jnp.float32(rope_base), exponents)
    angles = position_rows.astype(jnp.float32)[:, None] * inverse_freq[None, :]
    cosine_table = jnp.cos(angles)
    sine_table = jnp.sin(angles)
    return (jnp.concatenate([cosine_table, cosine_table], -1), jnp.concatenate([sine_table, sine_table], -1))

def rotate_forward(values, cosine_table, sine_table):
    half_size = values.shape[-1] // 2
    turned = jnp.concatenate([-values[..., half_size:], values[..., :half_size]], -1)
    return values * cosine_table + turned * sine_table

def rotate_back(gradient, cosine_table, sine_table):
    half_size = gradient.shape[-1] // 2
    scaled = gradient * sine_table
    turned = jnp.concatenate([scaled[..., half_size:], -scaled[..., :half_size]], -1)
    return gradient * cosine_table + turned

def contract(left_array, right_array, left_dim, right_dim):
    return lax.dot_general(left_array, right_array, (((left_dim,), (right_dim,)), ((), ())), preferred_element_type=jnp.float32)

def adamw_update(weight, gradient, first_moment, second, step_rate, decay_weight):
    first_new = beta_first * first_moment + (1.0 - beta_first) * gradient
    second_new = beta_second * second + (1.0 - beta_second) * gradient * gradient
    first_hat = first_new / (1.0 - beta_first ** ADAM_STEP)
    second_hat = second_new / (1.0 - beta_second ** ADAM_STEP)
    weight_new = weight - step_rate * (first_hat / (jnp.sqrt(second_hat) + adam_eps) + decay_weight * weight)
    return (weight_new, first_new, second_new)

def rms_forward(rows_f32, gain_low):
    inv_rms = lax.rsqrt(lax.optimization_barrier(jnp.mean(rows_f32 * rows_f32, -1)) + norm_eps)
    unit_rows = rows_f32 * inv_rms[:, None]
    normed = (unit_rows * gain_low.astype(jnp.float32)).astype(jnp.bfloat16)
    return (inv_rms, unit_rows, normed)

def rms_backward(residual_grad, normed_grad, inv_rms, unit_rows, gain_low):
    scaled = normed_grad * gain_low.astype(jnp.float32)
    return residual_grad + inv_rms[:, None] * (scaled - unit_rows * lax.optimization_barrier(jnp.mean(scaled * unit_rows, -1))[:, None])

def sequence_pass(token_rows, position_rows, cotangent, weights):
    gain16, query16, qbias16, keyval16, vbias16, output16, mgain16, gate16, up16, down16 = weights
    token_count = token_rows.shape[0]
    key_width = KV_HEADS * HEAD_DIM
    rows_f32 = token_rows.astype(jnp.float32)
    inv_rms, unit_rows, normed = rms_forward(rows_f32, gain16)
    query_raw = jnp.dot(normed, query16, preferred_element_type=jnp.float32) + qbias16.astype(jnp.float32)
    full_bias = jnp.concatenate([jnp.zeros((key_width,), jnp.float32), vbias16.astype(jnp.float32)], 0)
    keyval_raw = jnp.dot(normed, keyval16, preferred_element_type=jnp.float32) + full_bias
    cosine_table, sine_table = rotary_tables(position_rows, HEAD_DIM)
    cos_heads = cosine_table[:, None, :]
    sin_heads = sine_table[:, None, :]
    query_rot = rotate_forward(query_raw.reshape(token_count, HEADS, HEAD_DIM), cos_heads, sin_heads).astype(jnp.bfloat16)
    key_rot = rotate_forward(keyval_raw[:, :key_width].reshape(token_count, KV_HEADS, HEAD_DIM), cos_heads, sin_heads).astype(jnp.bfloat16)
    value_low = keyval_raw[:, key_width:].reshape(token_count, KV_HEADS, HEAD_DIM).astype(jnp.bfloat16)
    block_tokens = min(token_count, 512)
    if token_count % block_tokens != 0:
        block_tokens = token_count
    block_count = token_count // block_tokens
    score_scale = HEAD_DIM ** (-0.5)
    query_blocks = query_rot.reshape(block_count, block_tokens, HEADS, HEAD_DIM)
    position_blocks = position_rows.reshape(block_count, block_tokens)

    def group_scores(query_block, pos_block, group_index):
        query_rows = query_block[:, group_index * GROUP:(group_index + 1) * GROUP].reshape(block_tokens * GROUP, HEAD_DIM)
        query_pos = jnp.repeat(pos_block, GROUP)
        scores = contract(query_rows, key_rot[:, group_index], 1, 1) * score_scale
        allowed = position_rows[None, :] <= query_pos[:, None]
        return (query_rows, jnp.where(allowed, scores, masked_score), allowed)

    def forward_block(block_inputs):
        query_block, pos_block = block_inputs
        attended_parts = []
        log_parts = []
        for group_index in range(KV_HEADS):
            query_rows, scores, allowed = group_scores(query_block, pos_block, group_index)
            row_max = lax.optimization_barrier(jnp.max(scores, -1))
            row_sum = lax.optimization_barrier(jnp.sum(jnp.where(allowed, jnp.exp(scores - row_max[:, None]), 0.0), -1))
            log_total = row_max + jnp.log(row_sum)
            attn_probs = jnp.where(allowed, jnp.exp(scores - log_total[:, None]), 0.0).astype(jnp.bfloat16)
            attended_part = jnp.dot(attn_probs, value_low[:, group_index], preferred_element_type=jnp.float32).astype(jnp.bfloat16)
            attended_parts.append(attended_part.reshape(block_tokens, GROUP, HEAD_DIM))
            log_parts.append(log_total.reshape(block_tokens, GROUP))
        return (jnp.concatenate(attended_parts, 1), jnp.concatenate(log_parts, 1))
    attended, log_total = lax.map(forward_block, (query_blocks, position_blocks))
    attended_rows = attended.reshape(token_count, HEADS * HEAD_DIM)
    mixed = rows_f32 + jnp.dot(attended_rows, output16, preferred_element_type=jnp.float32)
    inv_mixed, unit_mixed, normed_mixed = rms_forward(mixed, mgain16)
    gate = jnp.dot(normed_mixed, gate16, preferred_element_type=jnp.float32)
    upper = jnp.dot(normed_mixed, up16, preferred_element_type=jnp.float32)
    sigmoid_gate = jax.nn.sigmoid(gate)
    activated = (gate * sigmoid_gate * upper).astype(jnp.bfloat16)
    layer_rows = (mixed + jnp.dot(activated, down16, preferred_element_type=jnp.float32)).astype(jnp.bfloat16)
    grad_down = contract(activated, cotangent, 0, 0)
    activated_grad = contract(cotangent, down16, 1, 1)
    gate_grad = (activated_grad * upper * sigmoid_gate * (1.0 + gate * (1.0 - sigmoid_gate))).astype(jnp.bfloat16)
    upper_grad = (activated_grad * gate * sigmoid_gate).astype(jnp.bfloat16)
    grad_gate = contract(normed_mixed, gate_grad, 0, 0)
    grad_up = contract(normed_mixed, upper_grad, 0, 0)
    normed_mixed_grad = contract(gate_grad, gate16, 1, 1) + contract(upper_grad, up16, 1, 1)
    grad_mgain = lax.optimization_barrier(jnp.sum(normed_mixed_grad * unit_mixed, 0))
    mixed_grad = rms_backward(cotangent.astype(jnp.float32), normed_mixed_grad, inv_mixed, unit_mixed, mgain16)
    mixed_low = mixed_grad.astype(jnp.bfloat16)
    grad_output = contract(attended_rows, mixed_low, 0, 0)
    dattended = contract(mixed_low, output16, 1, 1).astype(jnp.bfloat16).reshape(token_count, HEADS, HEAD_DIM)
    row_delta = lax.optimization_barrier(jnp.sum(dattended.astype(jnp.float32) * attended_rows.reshape(token_count, HEADS, HEAD_DIM).astype(jnp.float32), -1))
    grad_blocks = dattended.reshape(block_count, block_tokens, HEADS, HEAD_DIM)

    def backward_block(key_grads, block_inputs):
        query_block, pos_block, grad_block, log_block, delta_block = block_inputs
        query_parts = []
        key_parts = []
        value_parts = []
        for group_index in range(KV_HEADS):
            head_slice = slice(group_index * GROUP, (group_index + 1) * GROUP)
            query_rows, scores, allowed = group_scores(query_block, pos_block, group_index)
            log_rows = log_block[:, head_slice].reshape(block_tokens * GROUP)
            delta_rows = delta_block[:, head_slice].reshape(block_tokens * GROUP)
            grad_rows = grad_block[:, head_slice].reshape(block_tokens * GROUP, HEAD_DIM)
            attn_probs = jnp.where(allowed, jnp.exp(scores - log_rows[:, None]), 0.0)
            prob_grad = contract(grad_rows, value_low[:, group_index], 1, 1)
            score_grad = (attn_probs * (prob_grad - delta_rows[:, None]) * score_scale).astype(jnp.bfloat16)
            query_parts.append(jnp.dot(score_grad, key_rot[:, group_index], preferred_element_type=jnp.float32).reshape(block_tokens, GROUP, HEAD_DIM))
            key_parts.append(contract(score_grad, query_rows, 0, 0))
            value_parts.append(contract(attn_probs.astype(jnp.bfloat16), grad_rows, 0, 0))
        return (key_grads + jnp.concatenate(key_parts + value_parts, -1), jnp.concatenate(query_parts, 1))
    key_grads, query_rot_grad = lax.scan(backward_block, jnp.zeros((token_count, 2 * key_width), jnp.float32), (query_blocks, position_blocks, grad_blocks, log_total, row_delta.reshape(block_count, block_tokens, HEADS)))
    dquery = rotate_back(query_rot_grad.reshape(token_count, HEADS, HEAD_DIM), cos_heads, sin_heads).reshape(token_count, HEADS * HEAD_DIM)
    dkeyval = jnp.concatenate([rotate_back(key_grads[:, :key_width].reshape(token_count, KV_HEADS, HEAD_DIM), cos_heads, sin_heads).reshape(token_count, key_width), key_grads[:, key_width:]], -1)
    grad_qbias = lax.optimization_barrier(jnp.sum(dquery, 0))
    grad_vbias = lax.optimization_barrier(jnp.sum(key_grads[:, key_width:], 0))
    dquery_low = dquery.astype(jnp.bfloat16)
    dkeyval_low = dkeyval.astype(jnp.bfloat16)
    grad_query = contract(normed, dquery_low, 0, 0)
    grad_keyval = contract(normed, dkeyval_low, 0, 0)
    dnormed = contract(dquery_low, query16, 1, 1) + contract(dkeyval_low, keyval16, 1, 1)
    grad_gain = lax.optimization_barrier(jnp.sum(dnormed * unit_rows, 0))
    input_rows = rms_backward(mixed_grad, dnormed, inv_rms, unit_rows, gain16)
    return (layer_rows, input_rows, (grad_gain, grad_query, grad_qbias, grad_keyval, grad_vbias, grad_output, grad_mgain, grad_gate, grad_up, grad_down))

def reference(layer_input, positions, out_grad, norm_gain, query_proj, query_bias, keyval_proj, value_bias, output_proj, mlp_gain, gate_proj, up_proj, down_proj, norm_gain_mean, query_proj_mean, query_bias_mean, keyval_proj_mean, value_bias_mean, output_proj_mean, mlp_gain_mean, gate_proj_mean, up_proj_mean, down_proj_mean, norm_gain_square, query_proj_square, query_bias_square, keyval_proj_square, value_bias_square, output_proj_square, mlp_gain_square, gate_proj_square, up_proj_square, down_proj_square):
    masters = (norm_gain, query_proj, query_bias, keyval_proj, value_bias, output_proj, mlp_gain, gate_proj, up_proj, down_proj)
    first_moments = (norm_gain_mean, query_proj_mean, query_bias_mean, keyval_proj_mean, value_bias_mean, output_proj_mean, mlp_gain_mean, gate_proj_mean, up_proj_mean, down_proj_mean)
    second_moments = (norm_gain_square, query_proj_square, query_bias_square, keyval_proj_square, value_bias_square, output_proj_square, mlp_gain_square, gate_proj_square, up_proj_square, down_proj_square)
    settings = ((vector_rate, 0.0), (matrix_rate, decay_rate), (vector_rate, 0.0), (matrix_rate, decay_rate), (vector_rate, 0.0), (output_rate, decay_rate), (vector_rate, 0.0), (matrix_rate, decay_rate), (matrix_rate, decay_rate), (matrix_rate, decay_rate))
    weights = tuple((tensor.astype(jnp.bfloat16) for tensor in masters))
    output_list = []
    input_list = []
    totals = None
    for sequence_index in range(SEQS):
        layer_rows, input_rows, gradients = sequence_pass(layer_input[sequence_index], positions[sequence_index], out_grad[sequence_index], weights)
        output_list.append(layer_rows)
        input_list.append(input_rows)
        if totals is None:
            totals = gradients
        else:
            totals = tuple((earlier + later for earlier, later in zip(totals, gradients)))
    updated = [adamw_update(weight, gradient, first_moment, second, setting[0], setting[1]) for weight, gradient, first_moment, second, setting in zip(masters, totals, first_moments, second_moments, settings)]
    return (jnp.stack(output_list), jnp.stack(input_list)) + tuple(totals) + tuple((entry[0] for entry in updated)) + tuple((entry[1] for entry in updated)) + tuple((entry[2] for entry in updated))
```

```python
import functools

import jax
import jax.numpy as jnp
import numpy as np
from jax import lax
from jax.experimental import pallas as pl
from jax.experimental.pallas import tpu as pltpu
from jax.sharding import Mesh
from jax.sharding import PartitionSpec as P

HEAD_DIM = 64
HEADS = 14
KV_HEADS = 2
ADAM_STEP = 4
GROUP = 7
KEY_WIDTH = KV_HEADS * HEAD_DIM
WIDTH = HEADS * HEAD_DIM


norm_eps = 1e-06
rope_base = 1000000.0
beta_first = 0.9
beta_second = 0.95
adam_eps = 1e-08
matrix_rate = 0.03
output_rate = 0.6
vector_rate = 0.5
decay_rate = 0.1
masked_score = -1e30
f32 = jnp.float32
bf16 = jnp.bfloat16
DEPTH_PARTS = 4
KEY_CHUNK = 256
VMEM = pl.BlockSpec(memory_space=pltpu.VMEM)
SMEM = pl.BlockSpec(memory_space=pltpu.SMEM)
AXES = ("z", "t", "f")


def adamw_update(weight, gradient, first_moment, second, step_rate, decay_weight):
    first_new = beta_first * first_moment + (1.0 - beta_first) * gradient
    second_new = beta_second * second + (1.0 - beta_second) * gradient * gradient
    first_hat = first_new / (1.0 - beta_first**ADAM_STEP)
    second_hat = second_new / (1.0 - beta_second**ADAM_STEP)
    weight_new = weight - step_rate * (
        first_hat / (jnp.sqrt(second_hat) + adam_eps) + decay_weight * weight
    )
    return (weight_new, first_new, second_new)


def dot(left_array, right_array, left_dim, right_dim):
    return lax.dot_general(
        left_array,
        right_array,
        (((left_dim,), (right_dim,)), ((), ())),
        preferred_element_type=f32,
    )


def split_dot(left_f32, right_low, left_dim, right_dim):
    high = left_f32.astype(bf16)
    rest = left_f32 - high.astype(f32)
    middle = rest.astype(bf16)
    low = (rest - middle.astype(f32)).astype(bf16)
    return (
        dot(high, right_low, left_dim, right_dim)
        + dot(middle, right_low, left_dim, right_dim)
        + dot(low, right_low, left_dim, right_dim)
    )


class Plan:
    def __init__(self, mesh):
        self.seqs = mesh.shape["fsdp"]
        self.ctx = mesh.shape["ctx"]
        self.total = self.ctx * self.seqs
        self.depth = DEPTH_PARTS
        self.across = self.ctx // self.depth
        self.plane = self.across * self.seqs
        self.core = self.seqs
        self.deep = [self.plane * step for step in range(1, self.depth)]
        bits = [1 << bit for bit in range(self.plane.bit_length() - 1)]
        self.flat = [bit for bit in bits if bit != self.core]
        self.near = [bit for bit in self.flat if bit > self.core]

    def swap(self, block, mask):
        return lax.ppermute(block, AXES, [(i, i ^ mask) for i in range(self.total)])


def join(plan, block, mask, kind):
    return kind.concatenate([block, plan.swap(block, mask)], 0)


def gather_flat(plan, block, kind=jnp):
    half = block.shape[1] // 2
    first, last = block[None, :, :half], block[None, :, half:]
    for one, other in zip(plan.flat, plan.flat[::-1]):
        first, last = join(plan, first, one, kind), join(plan, last, other, kind)
    both = kind.stack([first, last])[None]
    return join(plan, both, plan.core, kind)


def keep_half(plan, block, mask):
    half = block.shape[0] // 2
    arrived = plan.swap(block[half:], mask)
    return (block[:half].astype(f32) + arrived.astype(f32)).astype(bf16)


def scatter_flat(plan, blocks):
    both = keep_half(plan, blocks, plan.core)[0]
    first, last = both[0], both[1]
    for one, other in zip(plan.flat[::-1], plan.flat):
        first, last = keep_half(plan, first, one), keep_half(plan, last, other)
    return jnp.concatenate([first[0], last[0]], 1)


def gather_deep(plan, block, kind=jnp):
    return kind.stack([block] + [plan.swap(block, mask) for mask in plan.deep])


def scatter_deep(plan, blocks):
    total = blocks[0].astype(f32)
    for step, mask in enumerate(plan.deep):
        total = total + plan.swap(blocks[step + 1], mask).astype(f32)
    return total


def gather_all(plan, block, kind=jnp):
    return gather_flat(plan, gather_deep(plan, block, kind), kind)


def scatter_all(plan, blocks):
    return scatter_deep(plan, scatter_flat(plan, blocks))


class Traced(Plan):
    def swap(self, block, mask):
        moved = block.copy()
        moved[..., 0] ^= mask
        return moved


def row_sources(mesh, rows):
    start = np.zeros((rows, 2), np.int32)
    start[:, 1] = np.arange(rows)
    return gather_all(Traced(mesh), start, np)


def gather_keys(plan, keys, values):
    rows, width = keys.shape
    first = keys[None]
    for mask in plan.near:
        first = join(plan, first, mask, jnp)
    last = gather_deep(plan, values)[:, None]
    first = gather_deep(plan, first)
    for mask in plan.near:
        last = jnp.concatenate([last, plan.swap(last, mask)], 1)
    first = join(plan, first[None], plan.core, jnp)
    last = join(plan, last[None], plan.core, jnp)
    return first.reshape(-1, rows, width), last.reshape(-1, values.shape[0], width)


def scatter_keys(plan, keys, values):
    rows, width = keys.shape[1:]
    order = (2, plan.depth, plan.across // 2, rows, width)
    first = keep_half(plan, keys.reshape(order), plan.core)[0]
    last = keep_half(plan, values.reshape(order), plan.core)[0]
    last = jnp.swapaxes(last, 0, 1)
    for mask in plan.near[::-1]:
        last = keep_half(plan, last, mask)
    first = scatter_deep(plan, first).astype(bf16)
    last = scatter_deep(plan, last[0])
    for mask in plan.near[::-1][:-1]:
        first = keep_half(plan, first, mask)
    half = first.shape[0] // 2
    first = first[0].astype(f32) + plan.swap(first[half:], plan.near[0])[0].astype(f32)
    return first, last


def rms(rows_f32):
    inverse = lax.rsqrt(jnp.mean(rows_f32 * rows_f32, -1, keepdims=True) + norm_eps)
    return inverse, rows_f32 * inverse


def turn(values, cosine, sine, sign):
    tile = 128
    lane = lax.broadcasted_iota(jnp.int32, (values.shape[0], tile), 1) % HEAD_DIM
    early = lane < HEAD_DIM // 2
    parts = []
    for start in range(0, values.shape[1], tile):
        part = values[:, start : start + tile]
        ahead = pltpu.roll(part, tile - HEAD_DIM // 2, 1)
        behind = pltpu.roll(part, HEAD_DIM // 2, 1)
        turned = jnp.where(early, -sign * ahead, sign * behind)
        parts.append(part * cosine + turned * sine)
    return jnp.concatenate(parts, 1) if len(parts) > 1 else parts[0]


def project_kernel(rows, gain, spread, weights, bias, cosine, sine, normed_out, query, key, value):
    unused, unit = rms(rows[...].astype(f32))
    normed = (unit * gain[...]).astype(bf16)
    placed = dot(normed, spread[...], 1, 0).astype(bf16)
    normed_out[...] = placed
    raw = dot(placed, weights[...], 1, 0) + bias[...]
    cos, sin = cosine[...], sine[...]
    query[...] = turn(raw[:, :WIDTH], cos, sin, 1.0).astype(bf16)
    key[...] = turn(raw[:, WIDTH : WIDTH + KEY_WIDTH], cos, sin, 1.0).astype(bf16)
    value[...] = raw[:, WIDTH + KEY_WIDTH :].astype(bf16)


def heads_of(ref, block, group, size):
    rows = pl.ds(block * size, size)
    first = group * GROUP * HEAD_DIM
    return jnp.concatenate(
        [ref[rows, first + h * HEAD_DIM : first + (h + 1) * HEAD_DIM] for h in range(GROUP)], 0
    )


def put_heads(ref, block, group, size, values):
    first = group * GROUP * HEAD_DIM
    for h in range(GROUP):
        ref[block * size : (block + 1) * size, first + h * HEAD_DIM : first + (h + 1) * HEAD_DIM] = (
            values[h * size : (h + 1) * size].astype(ref.dtype)
        )


def sort_keys(place, source, target, size, stride):
    def move(block, carry):
        where = place[block]
        start = pl.multiple_of((where // 2) * stride + (where % 2) * size, 16)
        target[pl.ds(pl.multiple_of(block * size, size), size), :] = source[pl.ds(start, size), :]
        return carry

    lax.fori_loop(0, target.shape[0] // size, move, 0)


def turn_over(source, target, chunk):
    def move(step, carry):
        start = pl.multiple_of(step * chunk, chunk)
        part = source[pl.ds(start, chunk), :].astype(f32)
        target[:, pl.ds(start, chunk)] = part.T.astype(bf16)
        return carry

    lax.fori_loop(0, source.shape[0] // chunk, move, 0)


def chunk_scores(sorted_keys, start, chunk, group, queries, block_at, size):
    keys = sorted_keys[pl.ds(start, chunk), group * HEAD_DIM : (group + 1) * HEAD_DIM]
    scores = dot(keys, queries, 1, 1) * HEAD_DIM ** (-0.5)
    key_pos = start + lax.broadcasted_iota(jnp.int32, scores.shape, 0)
    query_pos = block_at * size + lax.broadcasted_iota(jnp.int32, scores.shape, 1) % size
    return jnp.where(key_pos <= query_pos, scores, masked_score)


def chunk_count(block_at, size, chunk):
    return ((block_at + 1) * size + chunk - 1) // chunk


def attend_kernel(
    size, stride, chunk, place, mine, query, keys, values, attended, log_total,
    sorted_keys, sorted_values, values_over,
):
    sort_keys(place, keys, sorted_keys, size, stride)
    sort_keys(place, values, sorted_values, size, 2 * size)
    turn_over(sorted_values, values_over, chunk)
    columns = GROUP * size
    for block in range(2):
        block_at = mine[block]
        for group in range(KV_HEADS):
            queries = heads_of(query, block, group, size)

            def step(index, carry):
                top, total, accum = carry
                start = pl.multiple_of(index * chunk, chunk)
                scores = chunk_scores(sorted_keys, start, chunk, group, queries, block_at, size)
                new_top = jnp.maximum(top, jnp.max(scores, 0, keepdims=True))
                weights = jnp.exp(scores - new_top)
                scale = jnp.exp(top - new_top)
                total = total * scale + jnp.sum(weights, 0, keepdims=True)
                part = dot(
                    values_over[group * HEAD_DIM : (group + 1) * HEAD_DIM, pl.ds(start, chunk)],
                    weights.astype(bf16), 1, 0,
                )
                return new_top, total, accum * scale + part

            top, total, accum = lax.fori_loop(
                0, chunk_count(block_at, size, chunk), step,
                (
                    jnp.full((1, columns), masked_score, f32),
                    jnp.zeros((1, columns), f32),
                    jnp.zeros((HEAD_DIM, columns), f32),
                ),
            )
            put_heads(attended, block, group, size, (accum / total).T)
            row = block * KV_HEADS + group
            log_total[row : row + 1, :] = top + jnp.log(total)


def backward_kernel(
    size, stride, chunk, place, mine, query, keys, values, attended, attended_grad, log_total,
    query_grad, key_grad, value_grad,
    sorted_keys, sorted_values, keys_over, key_sums, value_sums,
):
    sort_keys(place, keys, sorted_keys, size, stride)
    sort_keys(place, values, sorted_values, size, 2 * size)
    turn_over(sorted_keys, keys_over, chunk)
    key_sums[...] = jnp.zeros_like(key_sums)
    value_sums[...] = jnp.zeros_like(value_sums)
    columns = GROUP * size
    for block in range(2):
        block_at = mine[block]
        for group in range(KV_HEADS):
            queries = heads_of(query, block, group, size)
            grads = heads_of(attended_grad, block, group, size)
            outs = heads_of(attended, block, group, size)
            delta = jnp.sum((grads.astype(f32) * outs.astype(f32)).T, 0, keepdims=True)
            row = block * KV_HEADS + group
            log_row = log_total[row : row + 1, :]

            def step(index, accum):
                start = pl.multiple_of(index * chunk, chunk)
                scores = chunk_scores(sorted_keys, start, chunk, group, queries, block_at, size)
                probs = jnp.exp(scores - log_row)
                own_values = sorted_values[
                    pl.ds(start, chunk), group * HEAD_DIM : (group + 1) * HEAD_DIM
                ]
                prob_grad = dot(own_values, grads, 1, 1)
                score_grad = (probs * (prob_grad - delta) * HEAD_DIM ** (-0.5)).astype(bf16)
                key_sums[group, pl.ds(start, chunk), :] += dot(score_grad, queries, 1, 0)
                value_sums[group, pl.ds(start, chunk), :] += dot(probs.astype(bf16), grads, 1, 0)
                return accum + dot(
                    keys_over[group * HEAD_DIM : (group + 1) * HEAD_DIM, pl.ds(start, chunk)],
                    score_grad, 1, 0,
                )

            accum = lax.fori_loop(
                0, chunk_count(block_at, size, chunk), step, jnp.zeros((HEAD_DIM, columns), f32)
            )
            put_heads(query_grad, block, group, size, accum.T)

    def move(block, carry):
        where = place[block]
        target = pl.ds(pl.multiple_of(where * size, size), size)
        source = pl.ds(pl.multiple_of(block * size, size), size)
        for sums, out in ((key_sums, key_grad), (value_sums, value_grad)):
            out[target, :] = jnp.concatenate(
                [sums[g, source, :] for g in range(KV_HEADS)], 1
            ).astype(out.dtype)
        return carry

    lax.fori_loop(0, key_grad.shape[0] // size, move, 0)


def mix_kernel(attended, spread, weights, rows, gain, placed_out, mixed_out, normed_out):
    placed = dot(attended[...], spread[...], 1, 0).astype(bf16)
    placed_out[...] = placed
    mixed = rows[...].astype(f32) + dot(placed, weights[...], 1, 0)
    mixed_out[...] = mixed
    unused, unit = rms(mixed)
    normed_out[...] = (unit * gain[...]).astype(bf16)


def rms_backward(residual, normed_grad, inverse, unit, gain):
    scaled = normed_grad * gain
    return residual + inverse * (scaled - unit * jnp.mean(scaled * unit, -1, keepdims=True))


def unmix_kernel(
    normed_grad, mixed, cotangent, gain, spread, weights,
    mixed_grad_out, mixed_low_out, attended_grad, gain_grad,
):
    inverse, unit = rms(mixed[...])
    grad = normed_grad[...].astype(f32)
    gain_grad[...] = jnp.sum(grad * unit, 0, keepdims=True)
    mixed_grad = rms_backward(cotangent[...].astype(f32), grad, inverse, unit, gain[...])
    mixed_grad_out[...] = mixed_grad
    mixed_low = mixed_grad.astype(bf16)
    mixed_low_out[...] = mixed_low
    placed = dot(mixed_low, weights[...], 1, 1).astype(bf16)
    attended_grad[...] = dot(placed, spread[...], 1, 1).astype(bf16)


def finish_kernel(
    query_grad, key_grad, value_grad, cosine, sine, rows, gain, spread, weights, mixed_grad,
    low_grad, input_grad, gain_grad, query_bias_grad, value_bias_grad,
):
    cos, sin = cosine[...], sine[...]
    dquery = turn(query_grad[...], cos, sin, -1.0)
    dkey = turn(key_grad[...], cos, sin, -1.0)
    dvalue = value_grad[...]
    query_bias_grad[...] = jnp.sum(dquery, 0, keepdims=True)
    value_bias_grad[...] = jnp.sum(dvalue, 0, keepdims=True)
    low = jnp.concatenate([dquery, dkey, dvalue], 1).astype(bf16)
    low_grad[...] = low
    normed_grad = split_dot(dot(low, weights[...], 1, 1), spread[...], 1, 1)
    inverse, unit = rms(rows[...].astype(f32))
    gain_grad[...] = jnp.sum(normed_grad * unit, 0, keepdims=True)
    input_grad[...] = rms_backward(mixed_grad[...], normed_grad, inverse, unit, gain[...])


def call(kernel, outs, scratch=(), scalars=0, name=None):
    return pl.pallas_call(
        kernel,
        out_shape=[jax.ShapeDtypeStruct(shape, kind) for shape, kind in outs],
        in_specs=None if scalars is None else scalars,
        out_specs=[VMEM] * len(outs),
        scratch_shapes=list(scratch),
        compiler_params=pltpu.CompilerParams(vmem_limit_bytes=56 * 1024 * 1024),
        name=name,
    )


def per_device(plan, mesh_sources, *arguments):
    layer_input, positions, out_grad = arguments[:3]
    masters, first_moments, second_moments = arguments[3:13], arguments[13:23], arguments[23:33]
    (
        norm_gain, query_proj, query_bias, keyval_proj, value_bias,
        output_proj, mlp_gain, gate_proj, up_proj, down_proj,
    ) = masters
    depth, plane, total = plan.depth, plan.plane, plan.total
    own = lax.axis_index(AXES)
    token_rows, position_rows, cotangent = layer_input[0], positions[0], out_grad[0]
    token_count = token_rows.shape[0]
    size = token_count // 2
    rows = query_proj.shape[0]
    vectors = (norm_gain, query_bias, value_bias, mlp_gain)
    vector_sizes = [vector.shape[0] for vector in vectors]
    vector_total = sum(vector_sizes)
    padded = -(-(rows + 1) // 16) * 16
    half = padded // 2
    qkv_width = query_proj.shape[1] + keyval_proj.shape[1]
    sources = mesh_sources(padded)
    flat_sources = sources.reshape(-1, 2)
    order = sources.shape[:-2]
    vector_half, vector_row = rows // half, rows % half
    vector_masks = sources[:, vector_half, ..., vector_row, 0].reshape(-1)

    packed = jnp.concatenate([vector.astype(bf16) for vector in vectors])
    spare = jnp.concatenate([packed, jnp.zeros((qkv_width - vector_total,), bf16)])
    block = jnp.concatenate(
        [
            jnp.concatenate([query_proj, keyval_proj], 1).astype(bf16),
            spare[None],
            jnp.zeros((padded - rows - 1, qkv_width), bf16),
        ],
        0,
    )
    qkv_blocks = gather_all(plan, block)
    qkv_low = qkv_blocks.reshape(-1, qkv_width)
    owner = own ^ jnp.asarray(flat_sources[:, 0])
    target = jnp.where(
        jnp.asarray(flat_sources[:, 1] < rows), owner * rows + jnp.asarray(flat_sources[:, 1]), -1
    )
    spread = (lax.broadcasted_iota(jnp.int32, (WIDTH, target.shape[0]), 0) == target[None]).astype(
        bf16
    )
    vector_owner = own ^ jnp.asarray(vector_masks)
    vector_turn = (
        lax.broadcasted_iota(jnp.int32, (total, total), 0) == vector_owner[None]
    ).astype(bf16)
    vector_rows = qkv_blocks[:, vector_half, ..., vector_row, :vector_total].reshape(
        total, vector_total
    )
    vector_rows = dot(vector_turn, vector_rows, 1, 0)
    whole_vectors = []
    offset = 0
    for length in vector_sizes:
        whole_vectors.append(vector_rows[:, offset : offset + length].reshape(1, total * length))
        offset = offset + length
    gain_row, query_bias_row, value_bias_row, mlp_gain_row = whole_vectors
    bias_row = jnp.concatenate(
        [query_bias_row, jnp.zeros((1, KEY_WIDTH), f32), value_bias_row], 1
    )
    output_block = jnp.concatenate(
        [output_proj.astype(bf16), jnp.zeros((padded - rows, WIDTH), bf16)], 0
    )

    hidden = down_proj.shape[0]
    slice_width = hidden * depth
    slice_padded = -(-slice_width // 128) * 128

    def by_slice(weight):
        parts = weight.astype(bf16).reshape(rows, depth, plane, hidden).transpose(2, 0, 1, 3)
        parts = parts.reshape(plane, rows, slice_width)
        return jnp.pad(parts, ((0, 0), (0, 0), (0, slice_padded - slice_width)))

    gate_up_parts = jnp.concatenate([by_slice(gate_proj), by_slice(up_proj)], 2)
    gate_up_rows = lax.all_to_all(gate_up_parts, ("t", "f"), split_axis=0, concat_axis=0, tiled=True)
    gate_up_low = lax.all_gather(gate_up_rows, "z", axis=0, tiled=True).reshape(
        WIDTH, 2 * slice_padded
    )
    down_low = lax.all_gather(down_proj.astype(bf16), "z", axis=0, tiled=True)
    down_low = jnp.pad(down_low, ((0, slice_padded - slice_width), (0, 0)))
    gate_low, up_low = gate_up_low[:, :slice_padded], gate_up_low[:, slice_padded:]

    exponents = jnp.arange(HEAD_DIM // 2, dtype=f32) * (-2.0 / HEAD_DIM)
    inverse_freq = jnp.tile(jnp.power(f32(rope_base), exponents), 4)
    angles = position_rows.astype(f32)[:, None] * inverse_freq[None, :]
    cosine, sine = jnp.cos(angles), jnp.sin(angles)

    count = target.shape[0]
    placed_normed, query_rot, key_rot, value_low = call(
        project_kernel,
        [
            ((token_count, count), bf16),
            ((token_count, WIDTH), bf16),
            ((token_count, KEY_WIDTH), bf16),
            ((token_count, KEY_WIDTH), bf16),
        ],
        scalars=[VMEM] * 7,
        name="project",
    )(token_rows, gain_row, spread, qkv_low, bias_row, cosine, sine)

    block_at = jnp.stack([position_rows[0], position_rows[size]]) // size
    numbers = jnp.pad(block_at.astype(bf16)[None], ((0, 15), (0, KEY_WIDTH - 2)))
    all_keys, all_values = gather_keys(plan, jnp.concatenate([key_rot, numbers], 0), value_low)
    all_blocks = all_keys[:, token_count, :2].astype(jnp.int32).reshape(-1)
    block_count = all_blocks.shape[0]
    slots = lax.broadcasted_iota(jnp.int32, (block_count, block_count), 1)
    place = jnp.sum(
        jnp.where(
            all_blocks[:, None] == slots,
            lax.broadcasted_iota(jnp.int32, (block_count, block_count), 0),
            0,
        ),
        0,
    )
    key_rows = block_count * size
    stride = all_keys.shape[1]
    all_keys = all_keys.reshape(-1, KEY_WIDTH)
    all_values = all_values.reshape(-1, KEY_WIDTH)
    chunk = KEY_CHUNK
    attended, log_total = call(
        functools.partial(attend_kernel, size, stride, chunk),
        [((token_count, WIDTH), bf16), ((2 * KV_HEADS, GROUP * size), f32)],
        scratch=[
            pltpu.VMEM((key_rows, KEY_WIDTH), bf16),
            pltpu.VMEM((key_rows, KEY_WIDTH), bf16),
            pltpu.VMEM((KEY_WIDTH, key_rows), bf16),
        ],
        scalars=[SMEM, SMEM] + [VMEM] * 3,
        name="attend",
    )(place, block_at, query_rot, all_keys, all_values)

    output_low = gather_all(plan, output_block).reshape(-1, WIDTH)
    placed_attended, mixed, normed_mixed = call(
        mix_kernel,
        [
            ((token_count, count), bf16),
            ((token_count, WIDTH), f32),
            ((token_count, WIDTH), bf16),
        ],
        scalars=[VMEM] * 5,
        name="mix",
    )(attended, spread, output_low, token_rows, mlp_gain_row)

    all_cotangent = gather_flat(plan, cotangent[None])
    token_order = all_cotangent.shape
    all_cotangent = all_cotangent.reshape(-1, WIDTH)
    all_normed = gather_flat(plan, normed_mixed[None]).reshape(-1, WIDTH)
    activated_grad = dot(all_cotangent, down_low, 1, 1)
    gate = dot(all_normed, gate_low, 1, 0)
    upper = dot(all_normed, up_low, 1, 0)
    sigmoid_gate = jax.nn.sigmoid(gate)
    gate_grad = (
        activated_grad * upper * sigmoid_gate * (1.0 + gate * (1.0 - sigmoid_gate))
    ).astype(bf16)
    upper_grad = (activated_grad * gate * sigmoid_gate).astype(bf16)
    activated = (gate * sigmoid_gate * upper).astype(bf16)
    normed_mixed_terms = dot(gate_grad, gate_low, 1, 1) + dot(upper_grad, up_low, 1, 1)
    normed_mixed_grad = scatter_flat(plan, normed_mixed_terms.astype(bf16).reshape(token_order))[0]
    layer_terms = dot(activated, down_low, 1, 0).astype(bf16)
    layer_rows = mixed + scatter_flat(plan, layer_terms.reshape(token_order))[0].astype(f32)
    layer_rows = layer_rows.astype(bf16)

    mixed_grad, mixed_low, attended_grad, part_mgain = call(
        unmix_kernel,
        [
            ((token_count, WIDTH), f32),
            ((token_count, WIDTH), bf16),
            ((token_count, WIDTH), bf16),
            ((1, WIDTH), f32),
        ],
        scalars=[VMEM] * 6,
        name="unmix",
    )(normed_mixed_grad, mixed, cotangent, mlp_gain_row, spread, output_low)

    part_gate = dot(all_normed, gate_grad, 0, 0).astype(bf16)
    part_up = dot(all_normed, upper_grad, 0, 0).astype(bf16)
    part_down = dot(activated, all_cotangent, 0, 0)[:slice_width].astype(bf16)
    gate_up_sum = lax.psum_scatter(
        jnp.concatenate([part_gate, part_up], 1), "z", scatter_dimension=0, tiled=True
    )
    down_sum = lax.psum_scatter(part_down, "z", scatter_dimension=0, tiled=True)
    gate_up_sum = lax.all_to_all(
        gate_up_sum.reshape(plane, rows, 2 * slice_padded),
        ("t", "f"), split_axis=0, concat_axis=0, tiled=True,
    )

    def from_slice(parts):
        parts = parts[:, :, :slice_width].reshape(plane, rows, depth, hidden)
        return parts.transpose(1, 2, 0, 3).reshape(rows, -1).astype(f32)

    grad_gate = from_slice(gate_up_sum[:, :, :slice_padded])
    grad_up = from_slice(gate_up_sum[:, :, slice_padded:])
    grad_down = down_sum.astype(f32)
    part_output = dot(placed_attended, mixed_low, 0, 0).astype(bf16)
    grad_output = scatter_all(plan, part_output.reshape(order + (half, WIDTH)))[:rows]

    query_rot_grad, key_terms, value_terms = call(
        functools.partial(backward_kernel, size, stride, chunk),
        [
            ((token_count, WIDTH), f32),
            ((key_rows, KEY_WIDTH), bf16),
            ((key_rows, KEY_WIDTH), bf16),
        ],
        scratch=[
            pltpu.VMEM((key_rows, KEY_WIDTH), bf16),
            pltpu.VMEM((key_rows, KEY_WIDTH), bf16),
            pltpu.VMEM((KEY_WIDTH, key_rows), bf16),
            pltpu.VMEM((KV_HEADS, key_rows, HEAD_DIM), f32),
            pltpu.VMEM((KV_HEADS, key_rows, HEAD_DIM), f32),
        ],
        scalars=[SMEM, SMEM] + [VMEM] * 6,
        name="backward",
    )(place, block_at, query_rot, all_keys, all_values, attended, attended_grad, log_total)
    key_sum, value_sum = scatter_keys(
        plan,
        key_terms.reshape(-1, token_count, KEY_WIDTH),
        value_terms.reshape(-1, token_count, KEY_WIDTH),
    )

    low_grad, input_rows, part_gain, part_qbias, part_vbias = call(
        finish_kernel,
        [
            ((token_count, qkv_width), bf16),
            ((token_count, WIDTH), f32),
            ((1, WIDTH), f32),
            ((1, WIDTH), f32),
            ((1, KEY_WIDTH), f32),
        ],
        scalars=[VMEM] * 10,
        name="finish",
    )(
        query_rot_grad, key_sum, value_sum, cosine, sine, token_rows, gain_row, spread,
        qkv_low, mixed_grad,
    )
    vector_parts = jnp.concatenate(
        [
            part.reshape(total, -1)
            for part in (part_gain, part_qbias, part_vbias, part_mgain)
        ],
        1,
    )
    vector_parts = split_dot(vector_parts, vector_turn, 0, 0).T
    spare_rows = jnp.pad(
        vector_parts.reshape((2, 1) + order[2:] + (1, vector_total)),
        (
            (0, 0), (vector_half, 1 - vector_half), (0, 0), (0, 0),
            (vector_row, half - 1 - vector_row), (0, qkv_width - vector_total),
        ),
    )
    part_qkv = dot(placed_normed, low_grad, 0, 0).reshape(order + (half, qkv_width)) + spare_rows
    qkv_sum = scatter_all(plan, part_qkv.astype(bf16))
    grad_query = qkv_sum[:rows, :WIDTH]
    grad_keyval = qkv_sum[:rows, WIDTH:]
    vector_sums = qkv_sum[rows]
    vector_grads = []
    offset = 0
    for length in vector_sizes:
        vector_grads.append(vector_sums[offset : offset + length])
        offset = offset + length
    grad_gain, grad_qbias, grad_vbias, grad_mgain = vector_grads
    gradients = (
        grad_gain, grad_query, grad_qbias, grad_keyval, grad_vbias,
        grad_output, grad_mgain, grad_gate, grad_up, grad_down,
    )
    vector, matrix = (vector_rate, 0.0), (matrix_rate, decay_rate)
    settings = (
        vector, matrix, vector, matrix, vector, (output_rate, decay_rate), vector,
        matrix, matrix, matrix,
    )
    updated = [
        adamw_update(weight, gradient, first_moment, second, setting[0], setting[1])
        for weight, gradient, first_moment, second, setting in zip(
            masters, gradients, first_moments, second_moments, settings
        )
    ]
    return (
        (layer_rows[None], input_rows[None])
        + tuple(gradients)
        + tuple((entry[0] for entry in updated))
        + tuple((entry[1] for entry in updated))
        + tuple((entry[2] for entry in updated))
    )


def solution(mesh):
    plan = Plan(mesh)
    devices = mesh.devices.reshape(plan.depth, plan.across, plan.seqs)
    return jax.shard_map(
        functools.partial(per_device, plan, functools.partial(row_sources, mesh)),
        mesh=Mesh(devices, AXES),
        in_specs=(
            P("f", ("z", "t"), None),
            P("f", ("z", "t")),
            P("f", ("z", "t"), None),
            P(AXES),
            P(AXES, None),
            P(AXES),
            P(AXES, None),
            P(AXES),
            P(AXES, None),
            P(AXES),
            P(AXES, None),
            P(AXES, None),
            P(AXES, None),
            P(AXES),
            P(AXES, None),
            P(AXES),
            P(AXES, None),
            P(AXES),
            P(AXES, None),
            P(AXES),
            P(AXES, None),
            P(AXES, None),
            P(AXES, None),
            P(AXES),
            P(AXES, None),
            P(AXES),
            P(AXES, None),
            P(AXES),
            P(AXES, None),
            P(AXES),
            P(AXES, None),
            P(AXES, None),
            P(AXES, None),
        ),
        out_specs=(
            P("f", ("z", "t"), None),
            P("f", ("z", "t"), None),
            P(AXES),
            P(AXES, None),
            P(AXES),
            P(AXES, None),
            P(AXES),
            P(AXES, None),
            P(AXES),
            P(AXES, None),
            P(AXES, None),
            P(AXES, None),
            P(AXES),
            P(AXES, None),
            P(AXES),
            P(AXES, None),
            P(AXES),
            P(AXES, None),
            P(AXES),
            P(AXES, None),
            P(AXES, None),
            P(AXES, None),
            P(AXES),
            P(AXES, None),
            P(AXES),
            P(AXES, None),
            P(AXES),
            P(AXES, None),
            P(AXES),
            P(AXES, None),
            P(AXES, None),
            P(AXES, None),
            P(AXES),
            P(AXES, None),
            P(AXES),
            P(AXES, None),
            P(AXES),
            P(AXES, None),
            P(AXES),
            P(AXES, None),
            P(AXES, None),
            P(AXES, None),
        ),
        check_vma=False,
    )
```

```python
import functools

import jax
import jax.numpy as jnp
import numpy as np
from jax import lax
from jax.experimental import pallas as pl
from jax.experimental.pallas import tpu as pltpu
from jax.sharding import Mesh
from jax.sharding import PartitionSpec as P

HEAD_DIM = 64
HEADS = 14
KV_HEADS = 2
ADAM_STEP = 4
GROUP = 7
KEY_WIDTH = KV_HEADS * HEAD_DIM
WIDTH = HEADS * HEAD_DIM


norm_eps = 1e-06
rope_base = 1000000.0
beta_first = 0.9
beta_second = 0.95
adam_eps = 1e-08
matrix_rate = 0.03
output_rate = 0.6
vector_rate = 0.5
decay_rate = 0.1
masked_score = -1e30
f32 = jnp.float32
bf16 = jnp.bfloat16
DEPTH_PARTS = 4
KEY_CHUNK = 256
LANES = 128
OUTPUT_LANES = slice(WIDTH + 2 * KEY_WIDTH, 2 * WIDTH + 2 * KEY_WIDTH)
VMEM = pl.BlockSpec(memory_space=pltpu.VMEM)
SMEM = pl.BlockSpec(memory_space=pltpu.SMEM)
AXES = ("z", "t", "f")


def adamw_update(weight, gradient, first_moment, second, step_rate, decay_weight):
    first_new = beta_first * first_moment + (1.0 - beta_first) * gradient
    second_new = beta_second * second + (1.0 - beta_second) * gradient * gradient
    first_hat = first_new / (1.0 - beta_first**ADAM_STEP)
    second_hat = second_new / (1.0 - beta_second**ADAM_STEP)
    weight_new = weight - step_rate * (
        first_hat / (jnp.sqrt(second_hat) + adam_eps) + decay_weight * weight
    )
    return (weight_new, first_new, second_new)


def dot(left_array, right_array, left_dim, right_dim):
    return lax.dot_general(
        left_array,
        right_array,
        (((left_dim,), (right_dim,)), ((), ())),
        preferred_element_type=f32,
    )


def split_dot(left_f32, right_low, left_dim, right_dim):
    high = left_f32.astype(bf16)
    rest = left_f32 - high.astype(f32)
    middle = rest.astype(bf16)
    low = (rest - middle.astype(f32)).astype(bf16)
    return (
        dot(high, right_low, left_dim, right_dim)
        + dot(middle, right_low, left_dim, right_dim)
        + dot(low, right_low, left_dim, right_dim)
    )


class Plan:
    def __init__(self, mesh):
        self.seqs = mesh.shape["fsdp"]
        self.ctx = mesh.shape["ctx"]
        self.total = self.ctx * self.seqs
        self.depth = DEPTH_PARTS
        self.across = self.ctx // self.depth
        self.plane = self.across * self.seqs
        self.core = self.seqs
        self.deep = [self.plane * step for step in range(1, self.depth)]
        bits = [1 << bit for bit in range(self.plane.bit_length() - 1)]
        self.flat = [bit for bit in bits if bit != self.core]
        self.near = [bit for bit in self.flat if bit > self.core]

    def swap(self, block, mask):
        return lax.ppermute(block, AXES, [(i, i ^ mask) for i in range(self.total)])


def join(plan, block, mask, kind):
    return kind.concatenate([block, plan.swap(block, mask)], 0)


def gather_flat(plan, block, kind=jnp):
    half = block.shape[1] // 2
    first, last = block[None, :, :half], block[None, :, half:]
    for one, other in zip(plan.flat, plan.flat[::-1]):
        first, last = join(plan, first, one, kind), join(plan, last, other, kind)
    both = kind.stack([first, last])
    return both, plan.swap(both, plan.core)


def keep_half(plan, block, mask):
    half = block.shape[0] // 2
    arrived = plan.swap(block[half:], mask)
    return (block[:half].astype(f32) + arrived.astype(f32)).astype(bf16)


def add_arrived(plan, kept, sent):
    return (kept.astype(f32) + plan.swap(sent, plan.core).astype(f32)).astype(bf16)


def scatter_flat(plan, blocks):
    return scatter_halves(plan, add_arrived(plan, *blocks))


def scatter_halves(plan, both):
    first, last = both[0], both[1]
    for one, other in zip(plan.flat[::-1], plan.flat):
        first, last = keep_half(plan, first, one), keep_half(plan, last, other)
    return jnp.concatenate([first[0], last[0]], 1)


def gather_deep(plan, block, kind=jnp):
    return kind.stack([block] + [plan.swap(block, mask) for mask in plan.deep])


def scatter_deep(plan, blocks):
    total = blocks[0].astype(f32)
    for step, mask in enumerate(plan.deep):
        total = total + plan.swap(blocks[step + 1], mask).astype(f32)
    return total


def spread_flat(plan, block):
    blocks = jnp.broadcast_to(block[None], (plan.plane,) + block.shape)
    return lax.all_to_all(blocks, ("t", "f"), split_axis=0, concat_axis=0, tiled=True)


def collect_flat(blocks):
    arrived = lax.all_to_all(blocks, ("t", "f"), split_axis=0, concat_axis=0, tiled=True)
    return jnp.sum(arrived.astype(f32), 0)


def after(value, earlier):
    return lax.optimization_barrier((value, earlier))[0]


class Traced(Plan):
    def swap(self, block, mask):
        moved = block.copy()
        moved[..., 0] ^= mask
        return moved


def row_sources(mesh, rows):
    start = np.zeros((rows, 2), np.int32)
    start[:, 1] = np.arange(rows)
    traced = Traced(mesh)
    return np.stack(gather_flat(traced, gather_deep(traced, start, np), np))


def token_sources(mesh):
    start = np.zeros((1, 2, 2), np.int32)
    start[:, :, 1] = np.arange(2)
    return np.stack(gather_flat(Traced(mesh), start, np)).reshape(-1, 2)


def gather_near(plan, block):
    block = block[None]
    for mask in plan.near:
        block = join(plan, block, mask, jnp)
    return block


def gather_keys(plan, block):
    block = gather_deep(plan, block)
    block = join(plan, block[None], plan.core, jnp)
    return block.reshape((-1,) + block.shape[-2:])


def scatter_keys(plan, blocks):
    order = (plan.depth, plan.across // 2, -1, blocks[0].shape[-1])
    blocks = add_arrived(plan, *blocks).reshape(order)
    blocks = jnp.swapaxes(blocks, 0, 1)
    for mask in plan.near[::-1]:
        blocks = keep_half(plan, blocks, mask)
    return scatter_deep(plan, blocks[0])


def rms(rows_f32):
    inverse = lax.rsqrt(jnp.mean(rows_f32 * rows_f32, -1, keepdims=True) + norm_eps)
    return inverse, rows_f32 * inverse


def turn(values, cosine, sine, sign):
    tile = 128
    lane = lax.broadcasted_iota(jnp.int32, (values.shape[0], tile), 1) % HEAD_DIM
    early = lane < HEAD_DIM // 2
    parts = []
    for start in range(0, values.shape[1], tile):
        part = values[:, start : start + tile]
        ahead = pltpu.roll(part, tile - HEAD_DIM // 2, 1)
        behind = pltpu.roll(part, HEAD_DIM // 2, 1)
        turned = jnp.where(early, -sign * ahead, sign * behind)
        parts.append(part * cosine + turned * sine)
    return jnp.concatenate(parts, 1) if len(parts) > 1 else parts[0]


def owned_by(owner, width, length):
    column = lax.broadcasted_iota(jnp.int32, (owner.shape[0], width), 1)
    return (column >= owner * length) & (column < (owner + 1) * length)


def lane_of(width, length, offset, lanes):
    entry = lax.broadcasted_iota(jnp.int32, (width, lanes), 0) % length
    lane = lax.broadcasted_iota(jnp.int32, (width, lanes), 1)
    return (lane == entry + offset).astype(bf16)


def times(left, first, last, lanes):
    half = first.shape[0]
    return dot(left[:, :half], first[:, lanes], 1, 0) + dot(left[:, half:], last[:, lanes], 1, 0)


def times_over(left, first, last, lanes):
    return jnp.concatenate(
        [dot(left, first[:, lanes], 1, 1), dot(left, last[:, lanes], 1, 1)], 1
    )


def project_kernel(
    sizes, rows, spread, marks, owner, first, last, cosine, sine,
    normed_out, query, key, value, gain_out, mlp_gain_out,
):
    lanes = slice(0, LANES)
    half = first.shape[0]
    spare = dot(marks[:half, :], first[:, lanes], 0, 0) + dot(marks[half:, :], last[:, lanes], 0, 0)
    spare = spare.astype(bf16)
    vectors, offset = [], 0
    for length, width in sizes:
        placed = dot(spare, lane_of(width, length, offset, LANES), 1, 1)
        mine = owned_by(owner[...], width, length)
        vectors.append(jnp.sum(jnp.where(mine, placed, 0.0), 0, keepdims=True))
        offset = offset + length
    gain, query_bias, value_bias, mlp_gain = vectors
    gain_out[...] = gain
    mlp_gain_out[...] = mlp_gain
    unused, unit = rms(rows[...].astype(f32))
    normed = (unit * gain).astype(bf16)
    placed = dot(normed, spread[...], 1, 0).astype(bf16)
    normed_out[...] = placed
    raw = times(placed, first, last, slice(0, WIDTH + 2 * KEY_WIDTH))
    cos, sin = cosine[...], sine[...]
    query[...] = turn(raw[:, :WIDTH] + query_bias, cos, sin, 1.0).astype(bf16)
    key[...] = turn(raw[:, WIDTH : WIDTH + KEY_WIDTH], cos, sin, 1.0).astype(bf16)
    value[...] = (raw[:, WIDTH + KEY_WIDTH :] + value_bias).astype(bf16)


def heads_of(ref, block, group, size):
    rows = pl.ds(block * size, size)
    first = group * GROUP * HEAD_DIM
    return jnp.concatenate(
        [ref[rows, first + h * HEAD_DIM : first + (h + 1) * HEAD_DIM] for h in range(GROUP)], 0
    )


def put_heads(ref, block, group, size, values):
    first = group * GROUP * HEAD_DIM
    for h in range(GROUP):
        ref[block * size : (block + 1) * size, first + h * HEAD_DIM : first + (h + 1) * HEAD_DIM] = (
            values[h * size : (h + 1) * size].astype(ref.dtype)
        )


def sort_keys(place, source, keys, values, size, stride):
    def move(block, carry):
        where = place[block]
        start = pl.multiple_of((where // 2) * stride + (where % 2) * size, 16)
        target = pl.ds(pl.multiple_of(block * size, size), size)
        keys[target, :] = source[pl.ds(start, size), :KEY_WIDTH]
        values[target, :] = source[pl.ds(start, size), KEY_WIDTH:]
        return carry

    lax.fori_loop(0, keys.shape[0] // size, move, 0)


def turn_over(source, target, chunk):
    def move(step, carry):
        start = pl.multiple_of(step * chunk, chunk)
        part = source[pl.ds(start, chunk), :].astype(f32)
        target[:, pl.ds(start, chunk)] = part.T.astype(bf16)
        return carry

    lax.fori_loop(0, source.shape[0] // chunk, move, 0)


def masked(scores, start, block_at, size):
    key_pos = start + lax.broadcasted_iota(jnp.int32, scores.shape, 0)
    query_pos = block_at * size + lax.broadcasted_iota(jnp.int32, scores.shape, 1) % size
    return jnp.where(key_pos <= query_pos, scores, masked_score)


def over_chunks(step, block_at, size, chunk, carry):
    whole = (block_at * size) // chunk
    carry = lax.fori_loop(0, whole, functools.partial(step, False), carry)
    return step(True, whole, carry)


def scaled_heads(ref, block, group, size):
    return heads_of(ref, block, group, size) * bf16(HEAD_DIM ** (-0.5))


def attend_kernel(
    size, stride, chunk, place, mine, query, keys, attended, log_total,
    sorted_keys, sorted_values, values_over,
):
    sort_keys(place, keys, sorted_keys, sorted_values, size, stride)
    turn_over(sorted_values, values_over, chunk)
    columns = GROUP * size
    for block in range(2):
        block_at = mine[block]
        queries = [scaled_heads(query, block, group, size) for group in range(KV_HEADS)]

        def step(last, index, carry):
            start = pl.multiple_of(index * chunk, chunk)
            result = []
            for group in range(KV_HEADS):
                top, total, accum = carry[group]
                lanes = slice(group * HEAD_DIM, (group + 1) * HEAD_DIM)
                scores = dot(sorted_keys[pl.ds(start, chunk), lanes], queries[group], 1, 1)
                if last:
                    scores = masked(scores, start, block_at, size)
                new_top = jnp.maximum(top, jnp.max(scores, 0, keepdims=True))
                weights = jnp.exp(scores - new_top)
                scale = jnp.exp(top - new_top)
                total = total * scale + jnp.sum(weights, 0, keepdims=True)
                part = dot(values_over[lanes, pl.ds(start, chunk)], weights.astype(bf16), 1, 0)
                result.append((new_top, total, accum * scale + part))
            return tuple(result)

        zero = (
            jnp.full((1, columns), masked_score, f32),
            jnp.zeros((1, columns), f32),
            jnp.zeros((HEAD_DIM, columns), f32),
        )
        carry = over_chunks(step, block_at, size, chunk, (zero,) * KV_HEADS)
        for group in range(KV_HEADS):
            top, total, accum = carry[group]
            put_heads(attended, block, group, size, (accum / total).T)
            row = block * KV_HEADS + group
            log_total[row : row + 1, :] = top + jnp.log(total)


def backward_kernel(
    size, stride, chunk, place, mine, query, keys, attended, attended_grad, log_total,
    query_grad, kept_grad, sent_grad,
    sorted_keys, sorted_values, keys_over, key_sums, value_sums,
):
    sort_keys(place, keys, sorted_keys, sorted_values, size, stride)
    turn_over(sorted_keys, keys_over, chunk)
    key_sums[...] = jnp.zeros_like(key_sums)
    value_sums[...] = jnp.zeros_like(value_sums)
    columns = GROUP * size
    for block in range(2):
        block_at = mine[block]
        queries, grads, deltas, logs = [], [], [], []
        for group in range(KV_HEADS):
            queries.append(scaled_heads(query, block, group, size))
            grad = heads_of(attended_grad, block, group, size)
            out = heads_of(attended, block, group, size)
            grads.append(grad)
            deltas.append(
                jnp.sum((grad.astype(f32) * out.astype(f32)).T, 0, keepdims=True)
            )
            row = block * KV_HEADS + group
            logs.append(log_total[row : row + 1, :])

        def step(last, index, carry):
            start = pl.multiple_of(index * chunk, chunk)
            result = []
            for group in range(KV_HEADS):
                lanes = slice(group * HEAD_DIM, (group + 1) * HEAD_DIM)
                rows = pl.ds(start, chunk)
                scores = dot(sorted_keys[rows, lanes], queries[group], 1, 1)
                if last:
                    scores = masked(scores, start, block_at, size)
                probs = jnp.exp(scores - logs[group])
                prob_grad = dot(sorted_values[rows, lanes], grads[group], 1, 1)
                score_grad = (probs * (prob_grad - deltas[group])).astype(bf16)
                key_sums[group, rows, :] += dot(score_grad, queries[group], 1, 0)
                value_sums[group, rows, :] += dot(probs.astype(bf16), grads[group], 1, 0)
                result.append(carry[group] + dot(keys_over[lanes, rows], score_grad, 1, 0))
            return tuple(result)

        zero = jnp.zeros((HEAD_DIM, columns), f32)
        carry = over_chunks(step, block_at, size, chunk, (zero,) * KV_HEADS)
        for group in range(KV_HEADS):
            put_heads(query_grad, block, group, size, carry[group].T * HEAD_DIM ** (-0.5))

    span = kept_grad.shape[0] // size

    def move(block, carry):
        where = place[block]
        target = pl.ds(pl.multiple_of((where % span) * size, size), size)
        source = pl.ds(pl.multiple_of(block * size, size), size)
        total = jnp.concatenate(
            [sums[g, source, :] for sums in (key_sums, value_sums) for g in range(KV_HEADS)], 1
        ).astype(bf16)

        @pl.when(where < span)
        def keep():
            kept_grad[target, :] = total

        @pl.when(where >= span)
        def send():
            sent_grad[target, :] = total

        return carry

    lax.fori_loop(0, 2 * span, move, 0)


def pack_kernel(query, keyval, output, spare, packed):
    rows, width = query.shape
    side = keyval.shape[1]
    empty = packed.shape[0] - rows
    packed[:, :width] = jnp.concatenate([query[...], jnp.broadcast_to(spare[:, :width], (empty, width))], 0).astype(bf16)
    packed[:, width : width + side] = jnp.concatenate(
        [keyval[...], jnp.zeros((empty, side), f32)], 0
    ).astype(bf16)
    packed[:, width + side :] = jnp.concatenate(
        [output[...], jnp.zeros((empty, output.shape[1]), f32)], 0
    ).astype(bf16)


def feed_kernel(
    size, group, places, first, last, cotangent, gate_up, down,
    kept_grad, sent_grad, layer_terms, activated_out, hidden_grad,
):
    width = down.shape[0]
    halves = ((first, kept_grad), (last, sent_grad))
    count = first.shape[0] // (group * size)

    def step(side, index, carry):
        normed, normed_grad = halves[side]
        rows = pl.ds(pl.multiple_of(index * group * size, size), group * size)
        at = side * count + index
        all_rows = pl.ds(pl.multiple_of(at * group * size, size), group * size)
        spots = [
            pl.ds(pl.multiple_of(places[at * group + part] * size, size), size)
            for part in range(group)
        ]
        tokens = normed[rows, :]
        outs = jnp.concatenate([cotangent[spot, :] for spot in spots], 0)
        gate = dot(tokens, gate_up[:, :width], 1, 0)
        upper = dot(tokens, gate_up[:, width:], 1, 0)
        activated_grad = dot(outs, down[...], 1, 1)
        sigmoid = 1.0 / (1.0 + jnp.exp(-gate))
        silu = gate * sigmoid
        activated = (silu * upper).astype(bf16)
        gate_grad = (activated_grad * upper * sigmoid * (1.0 + gate * (1.0 - sigmoid))).astype(bf16)
        upper_grad = (activated_grad * silu).astype(bf16)
        hidden_grad[all_rows, :width] = gate_grad
        hidden_grad[all_rows, width:] = upper_grad
        normed_grad[rows, :] = (
            dot(gate_grad, gate_up[:, :width], 1, 1) + dot(upper_grad, gate_up[:, width:], 1, 1)
        ).astype(bf16)
        terms = dot(activated, down[...], 1, 0).astype(bf16)
        for part, spot in enumerate(spots):
            layer_terms[spot, :] = terms[part * size : (part + 1) * size]
            activated_out[spot, :] = activated[part * size : (part + 1) * size]
        return carry

    for side in range(2):
        lax.fori_loop(0, count, functools.partial(step, side), 0)


def mix_kernel(attended, spread, first, last, rows, gain, placed_out, mixed_out, normed_out):
    placed = dot(attended[...], spread[...], 1, 0).astype(bf16)
    placed_out[...] = placed
    mixed = rows[...].astype(f32) + times(placed, first, last, OUTPUT_LANES)
    mixed_out[...] = mixed
    unused, unit = rms(mixed)
    normed_out[...] = (unit * gain[...]).astype(bf16)


def rms_backward(residual, normed_grad, inverse, unit, gain):
    scaled = normed_grad * gain
    return residual + inverse * (scaled - unit * jnp.mean(scaled * unit, -1, keepdims=True))


def unmix_kernel(
    normed_grad, mixed, cotangent, gain, spread, first, last,
    mixed_grad_out, mixed_low_out, attended_grad, gain_grad,
):
    inverse, unit = rms(mixed[...])
    grad = normed_grad[...].astype(f32)
    gain_grad[...] = jnp.sum(grad * unit, 0, keepdims=True)
    mixed_grad = rms_backward(cotangent[...].astype(f32), grad, inverse, unit, gain[...])
    mixed_grad_out[...] = mixed_grad
    mixed_low = mixed_grad.astype(bf16)
    mixed_low_out[...] = mixed_low
    placed = times_over(mixed_low, first, last, OUTPUT_LANES).astype(bf16)
    attended_grad[...] = dot(placed, spread[...], 1, 1).astype(bf16)


def finish_kernel(
    sizes, query_grad, key_grad, cosine, sine, rows, gain, spread, marks, owner, first, last,
    placed_normed, mixed_grad, mlp_gain_grad,
    input_grad, part_first, part_last,
):
    cos, sin = cosine[...], sine[...]
    dquery = turn(query_grad[...], cos, sin, -1.0)
    dkey = turn(key_grad[:, :KEY_WIDTH], cos, sin, -1.0)
    dvalue = key_grad[:, KEY_WIDTH:]
    low = jnp.concatenate([dquery, dkey, dvalue], 1).astype(bf16)
    normed_grad = split_dot(
        times_over(low, first, last, slice(0, WIDTH + 2 * KEY_WIDTH)), spread[...], 1, 1
    )
    inverse, unit = rms(rows[...].astype(f32))
    input_grad[...] = rms_backward(mixed_grad[...], normed_grad, inverse, unit, gain[...])
    vectors = (
        jnp.sum(normed_grad * unit, 0, keepdims=True),
        jnp.sum(dquery, 0, keepdims=True),
        jnp.sum(dvalue, 0, keepdims=True),
        mlp_gain_grad[...],
    )
    spare, offset = jnp.zeros((owner.shape[0], LANES), f32), 0
    for (length, width), vector in zip(sizes, vectors):
        mine = jnp.where(owned_by(owner[...], width, length), vector, 0.0)
        spare = spare + split_dot(mine, lane_of(width, length, offset, LANES), 1, 0)
        offset = offset + length
    half = first.shape[0]
    over = placed_normed[...].astype(f32).T.astype(bf16)
    for at, out in ((0, part_first), (half, part_last)):
        part = dot(over[at : at + half], low, 1, 0)
        out[:, :LANES] = (
            part[:, :LANES] + dot(marks[at : at + half, :], spare.astype(bf16), 1, 0)
        ).astype(bf16)
        out[:, LANES:] = part[:, LANES:].astype(bf16)


def call(kernel, outs, scratch=(), scalars=0, name=None, cost=1):
    return pl.pallas_call(
        kernel,
        out_shape=[jax.ShapeDtypeStruct(shape, kind) for shape, kind in outs],
        in_specs=None if scalars is None else scalars,
        out_specs=[VMEM] * len(outs),
        scratch_shapes=list(scratch),
        compiler_params=pltpu.CompilerParams(vmem_limit_bytes=56 * 1024 * 1024),
        cost_estimate=pl.CostEstimate(
            flops=cost * 1_000_000_000, bytes_accessed=cost * 3_000_000, transcendentals=0
        ),
        name=name,
    )


def per_device(plan, mesh_sources, token_sources_of, *arguments):
    layer_input, positions, out_grad = arguments[:3]
    masters, first_moments, second_moments = arguments[3:13], arguments[13:23], arguments[23:33]
    (
        norm_gain, query_proj, query_bias, keyval_proj, value_bias,
        output_proj, mlp_gain, gate_proj, up_proj, down_proj,
    ) = masters
    depth, plane, total = plan.depth, plan.plane, plan.total
    own = lax.axis_index(AXES)
    token_rows, position_rows, cotangent = layer_input[0], positions[0], out_grad[0]
    token_count = token_rows.shape[0]
    size = token_count // 2
    rows = query_proj.shape[0]
    vectors = (norm_gain, query_bias, value_bias, mlp_gain)
    vector_sizes = [vector.shape[0] for vector in vectors]
    vector_total = sum(vector_sizes)
    padded = -(-(rows + 1) // 16) * 16
    half = padded // 2
    qkv_width = query_proj.shape[1] + keyval_proj.shape[1]
    sources = mesh_sources(padded)
    flat_sources = sources.reshape(-1, 2)
    order = sources.shape[:-2]
    vector_masks = flat_sources[flat_sources[:, 1] == rows, 0]

    packed = jnp.concatenate(vectors)[None]
    spare = jnp.pad(packed, ((0, 0), (0, WIDTH - vector_total)))
    (block,) = call(
        pack_kernel,
        [((padded, qkv_width + WIDTH), bf16)],
        scalars=[VMEM] * 4,
        name="pack",
        cost=2,
    )(query_proj, keyval_proj, output_proj, spare)
    deep_blocks = gather_deep(plan, block)
    hidden = down_proj.shape[0]
    slice_width = hidden * depth
    slice_padded = -(-slice_width // 128) * 128

    def by_slice(weight):
        parts = weight.astype(bf16).reshape(rows, depth, plane, hidden).transpose(2, 0, 1, 3)
        parts = parts.reshape(plane, rows, slice_width)
        return jnp.pad(parts, ((0, 0), (0, 0), (0, slice_padded - slice_width)))

    gate_up_parts = jnp.concatenate([by_slice(gate_proj), by_slice(up_proj)], 2)
    gate_up_rows = lax.all_to_all(gate_up_parts, ("t", "f"), split_axis=0, concat_axis=0, tiled=True)
    gate_up_low = lax.all_gather(
        gate_up_rows.reshape(plane * rows, 2 * slice_padded), "z", axis=0, tiled=True
    )
    down_low = lax.all_gather(down_proj.astype(bf16), "z", axis=0, tiled=True)
    down_low = jnp.pad(down_low, ((0, slice_padded - slice_width), (0, 0)))
    deep_blocks = after(deep_blocks, gate_up_rows)
    weights = [
        blocks.reshape(-1, qkv_width + WIDTH) for blocks in gather_flat(plan, deep_blocks)
    ]
    owner = own ^ jnp.asarray(flat_sources[:, 0])
    target = jnp.where(
        jnp.asarray(flat_sources[:, 1] < rows), owner * rows + jnp.asarray(flat_sources[:, 1]), -1
    )
    count = target.shape[0]
    column = lax.broadcasted_iota(jnp.int32, (WIDTH, count), 0)
    spread = (column == target[None]).astype(bf16)
    place_own = own % plane
    vector_owner = (own ^ jnp.asarray(vector_masks))[:, None]
    vector_at = flat_sources[:, 1] == rows
    marks = jnp.asarray(
        (np.flatnonzero(vector_at)[None] == np.arange(len(vector_at))[:, None]).astype(np.float32)
    ).astype(bf16)
    sizes = [(length, length * total) for length in vector_sizes]

    exponents = jnp.arange(HEAD_DIM // 2, dtype=f32) * (-2.0 / HEAD_DIM)
    inverse_freq = jnp.tile(jnp.power(f32(rope_base), exponents), 4)
    angles = position_rows.astype(f32)[:, None] * inverse_freq[None, :]
    cosine, sine = jnp.cos(angles), jnp.sin(angles)

    placed_normed, query_rot, key_rot, value_low, gain_row, mlp_gain_row = call(
        functools.partial(project_kernel, sizes),
        [
            ((token_count, count), bf16),
            ((token_count, WIDTH), bf16),
            ((token_count, KEY_WIDTH), bf16),
            ((token_count, KEY_WIDTH), bf16),
            ((1, WIDTH), f32),
            ((1, WIDTH), f32),
        ],
        scalars=[VMEM] * 8,
        name="project",
        cost=5,
    )(token_rows, spread, marks, vector_owner, *weights, cosine, sine)

    block_at = lax.div(
        jnp.stack([position_rows[0], position_rows[size]]), jnp.full((2,), size, jnp.int32)
    )
    numbers = jnp.pad(block_at.astype(bf16)[None], ((0, 15), (0, KEY_WIDTH - 2)))
    own_keys = jnp.concatenate(
        [jnp.concatenate([key_rot, value_low], 1), jnp.pad(numbers, ((0, 0), (0, KEY_WIDTH)))], 0
    )
    near_keys = gather_near(plan, own_keys)
    all_cotangent = spread_flat(plan, after(cotangent, near_keys)).reshape(-1, WIDTH)
    all_keys = gather_keys(plan, near_keys)
    all_blocks = all_keys[:, token_count, :2].astype(jnp.int32).reshape(-1)
    block_count = all_blocks.shape[0]
    slots = lax.broadcasted_iota(jnp.int32, (block_count, block_count), 1)
    place = jnp.sum(
        jnp.where(
            all_blocks[:, None] == slots,
            lax.broadcasted_iota(jnp.int32, (block_count, block_count), 0),
            0,
        ),
        0,
    )
    key_rows = block_count * size
    stride = all_keys.shape[1]
    all_keys = all_keys.reshape(-1, 2 * KEY_WIDTH)
    chunk = KEY_CHUNK
    attended, log_total = call(
        functools.partial(attend_kernel, size, stride, chunk),
        [((token_count, WIDTH), bf16), ((2 * KV_HEADS, GROUP * size), f32)],
        scratch=[
            pltpu.VMEM((key_rows, KEY_WIDTH), bf16),
            pltpu.VMEM((key_rows, KEY_WIDTH), bf16),
            pltpu.VMEM((KEY_WIDTH, key_rows), bf16),
        ],
        scalars=[SMEM, SMEM] + [VMEM] * 2,
        name="attend",
        cost=12,
    )(place, block_at, query_rot, all_keys)

    placed_attended, mixed, normed_mixed = call(
        mix_kernel,
        [
            ((token_count, count), bf16),
            ((token_count, WIDTH), f32),
            ((token_count, WIDTH), bf16),
        ],
        scalars=[VMEM] * 6,
        name="mix",
        cost=4,
    )(attended, spread, *weights, token_rows, mlp_gain_row)

    normed_blocks = gather_flat(plan, after(normed_mixed, all_cotangent)[None])
    token_order = normed_blocks[0].shape
    normed_blocks = [blocks.reshape(-1, WIDTH) for blocks in normed_blocks]
    token_total = 2 * normed_blocks[0].shape[0]
    moves = jnp.asarray(token_sources_of)
    places = (place_own ^ moves[:, 0]) * 2 + moves[:, 1]
    kept_terms, sent_terms, layer_terms, activated, hidden_grad = call(
        functools.partial(feed_kernel, size, 4),
        [
            ((token_total // 2, WIDTH), bf16),
            ((token_total // 2, WIDTH), bf16),
            ((token_total, WIDTH), bf16),
            ((token_total, slice_padded), bf16),
            ((token_total, 2 * slice_padded), bf16),
        ],
        scalars=[SMEM] + [VMEM] * 5,
        name="feed",
        cost=16,
    )(places, *normed_blocks, all_cotangent, gate_up_low, down_low)
    normed_mixed_grad = scatter_flat(
        plan, (kept_terms.reshape(token_order), sent_terms.reshape(token_order))
    )[0]

    mixed_grad, mixed_low, attended_grad, part_mgain = call(
        unmix_kernel,
        [
            ((token_count, WIDTH), f32),
            ((token_count, WIDTH), bf16),
            ((token_count, WIDTH), bf16),
            ((1, WIDTH), f32),
        ],
        scalars=[VMEM] * 7,
        name="unmix",
        cost=5,
    )(normed_mixed_grad, mixed, cotangent, mlp_gain_row, spread, *weights)

    split = token_total // 2
    part_gate_up = (
        dot(normed_blocks[0], hidden_grad[:split], 0, 0)
        + dot(normed_blocks[1], hidden_grad[split:], 0, 0)
    ).astype(bf16)
    part_down = dot(activated, all_cotangent, 0, 0)[:slice_width].astype(bf16)
    gate_up_sum = lax.psum_scatter(part_gate_up, "z", scatter_dimension=0, tiled=True)
    down_sum = lax.psum_scatter(
        after(part_down, gate_up_sum), "z", scatter_dimension=0, tiled=True
    )
    layer_terms = after(layer_terms, normed_mixed_grad).reshape(plane, token_count, WIDTH)
    layer_terms = lax.all_to_all(layer_terms, ("t", "f"), split_axis=0, concat_axis=0, tiled=True)
    layer_rows = (mixed + jnp.sum(layer_terms.astype(f32), 0)).astype(bf16)

    part_output = dot(placed_attended, mixed_low, 0, 0).astype(bf16)
    part_output = part_output.reshape(order + (half, WIDTH))
    part_output = add_arrived(plan, part_output[0], part_output[1])
    query_rot_grad, *key_terms = call(
        functools.partial(backward_kernel, size, stride, chunk),
        [
            ((token_count, WIDTH), f32),
            ((key_rows // 2, 2 * KEY_WIDTH), bf16),
            ((key_rows // 2, 2 * KEY_WIDTH), bf16),
        ],
        scratch=[
            pltpu.VMEM((key_rows, KEY_WIDTH), bf16),
            pltpu.VMEM((key_rows, KEY_WIDTH), bf16),
            pltpu.VMEM((KEY_WIDTH, key_rows), bf16),
            pltpu.VMEM((KV_HEADS, key_rows, HEAD_DIM), f32),
            pltpu.VMEM((KV_HEADS, key_rows, HEAD_DIM), f32),
        ],
        scalars=[SMEM, SMEM] + [VMEM] * 5,
        name="backward",
        cost=16,
    )(place, block_at, query_rot, all_keys, attended, attended_grad, log_total)
    key_terms = after(key_terms, layer_terms)
    key_sum = scatter_keys(plan, key_terms)

    key_sum = after(key_sum, gate_up_sum)
    gate_up_sum = lax.all_to_all(
        gate_up_sum.reshape(plane, rows, 2 * slice_padded),
        ("t", "f"), split_axis=0, concat_axis=0, tiled=True,
    )
    input_rows, *part_qkv = call(
        functools.partial(finish_kernel, sizes),
        [
            ((token_count, WIDTH), f32),
            ((count // 2, qkv_width), bf16),
            ((count // 2, qkv_width), bf16),
        ],
        scalars=[VMEM] * 14,
        name="finish",
        cost=9,
    )(
        query_rot_grad, key_sum, cosine, sine, token_rows, gain_row, spread, marks, vector_owner,
        *weights, placed_normed, mixed_grad, part_mgain,
    )
    part_qkv = [part.reshape(order[1:] + (half, qkv_width)) for part in part_qkv]
    part_qkv = add_arrived(plan, part_qkv[0], after(part_qkv[1], gate_up_sum))
    gate_up_sum = after(gate_up_sum, part_qkv)
    weight_sums = scatter_halves(plan, jnp.concatenate([part_qkv, part_output], -1))
    weight_sums = scatter_deep(plan, weight_sums)
    qkv_sum = weight_sums[:, :qkv_width]
    grad_output = weight_sums[:rows, qkv_width:]

    def from_slice(parts):
        parts = parts[:, :, :slice_width].reshape(plane, rows, depth, hidden)
        return parts.transpose(1, 2, 0, 3).reshape(rows, -1).astype(f32)

    grad_gate = from_slice(gate_up_sum[:, :, :slice_padded])
    grad_up = from_slice(gate_up_sum[:, :, slice_padded:])
    grad_down = down_sum.astype(f32)
    grad_query = qkv_sum[:rows, :WIDTH]
    grad_keyval = qkv_sum[:rows, WIDTH:]
    vector_sums = qkv_sum[rows]
    vector_grads = []
    offset = 0
    for length in vector_sizes:
        vector_grads.append(vector_sums[offset : offset + length])
        offset = offset + length
    grad_gain, grad_qbias, grad_vbias, grad_mgain = vector_grads
    gradients = (
        grad_gain, grad_query, grad_qbias, grad_keyval, grad_vbias,
        grad_output, grad_mgain, grad_gate, grad_up, grad_down,
    )
    vector, matrix = (vector_rate, 0.0), (matrix_rate, decay_rate)
    settings = (
        vector, matrix, vector, matrix, vector, (output_rate, decay_rate), vector,
        matrix, matrix, matrix,
    )
    updated = [
        adamw_update(weight, gradient, first_moment, second, setting[0], setting[1])
        for weight, gradient, first_moment, second, setting in zip(
            masters, gradients, first_moments, second_moments, settings
        )
    ]
    return (
        (layer_rows[None], input_rows[None])
        + tuple(gradients)
        + tuple((entry[0] for entry in updated))
        + tuple((entry[1] for entry in updated))
        + tuple((entry[2] for entry in updated))
    )


def solution(mesh):
    plan = Plan(mesh)
    devices = mesh.devices.reshape(plan.depth, plan.across, plan.seqs)
    return jax.shard_map(
        functools.partial(
            per_device, plan, functools.partial(row_sources, mesh), token_sources(mesh)
        ),
        mesh=Mesh(devices, AXES),
        in_specs=(
            P("f", ("z", "t"), None),
            P("f", ("z", "t")),
            P("f", ("z", "t"), None),
            P(AXES),
            P(AXES, None),
            P(AXES),
            P(AXES, None),
            P(AXES),
            P(AXES, None),
            P(AXES),
            P(AXES, None),
            P(AXES, None),
            P(AXES, None),
            P(AXES),
            P(AXES, None),
            P(AXES),
            P(AXES, None),
            P(AXES),
            P(AXES, None),
            P(AXES),
            P(AXES, None),
            P(AXES, None),
            P(AXES, None),
            P(AXES),
            P(AXES, None),
            P(AXES),
            P(AXES, None),
            P(AXES),
            P(AXES, None),
            P(AXES),
            P(AXES, None),
            P(AXES, None),
            P(AXES, None),
        ),
        out_specs=(
            P("f", ("z", "t"), None),
            P("f", ("z", "t"), None),
            P(AXES),
            P(AXES, None),
            P(AXES),
            P(AXES, None),
            P(AXES),
            P(AXES, None),
            P(AXES),
            P(AXES, None),
            P(AXES, None),
            P(AXES, None),
            P(AXES),
            P(AXES, None),
            P(AXES),
            P(AXES, None),
            P(AXES),
            P(AXES, None),
            P(AXES),
            P(AXES, None),
            P(AXES, None),
            P(AXES, None),
            P(AXES),
            P(AXES, None),
            P(AXES),
            P(AXES, None),
            P(AXES),
            P(AXES, None),
            P(AXES),
            P(AXES, None),
            P(AXES, None),
            P(AXES, None),
            P(AXES),
            P(AXES, None),
            P(AXES),
            P(AXES, None),
            P(AXES),
            P(AXES, None),
            P(AXES),
            P(AXES, None),
            P(AXES, None),
            P(AXES, None),
        ),
        check_vma=False,
    )
```

```python
import functools

import jax
import jax.numpy as jnp
import numpy as np
from jax import lax
from jax.experimental import pallas as pl
from jax.experimental.pallas import tpu as pltpu
from jax.sharding import Mesh
from jax.sharding import PartitionSpec as P

HEAD_DIM = 64
HEADS = 14
KV_HEADS = 2
ADAM_STEP = 4
GROUP = 7
KEY_WIDTH = KV_HEADS * HEAD_DIM
WIDTH = HEADS * HEAD_DIM


norm_eps = 1e-06
rope_base = 1000000.0
beta_first = 0.9
beta_second = 0.95
adam_eps = 1e-08
matrix_rate = 0.03
output_rate = 0.6
vector_rate = 0.5
decay_rate = 0.1
masked_score = -1e30
f32 = jnp.float32
bf16 = jnp.bfloat16
DEPTH_PARTS = 4
KEY_CHUNK = 512
LANES = 128
VMEM = pl.BlockSpec(memory_space=pltpu.VMEM)
SMEM = pl.BlockSpec(memory_space=pltpu.SMEM)
AXES = ("z", "t", "f")


def adamw_update(weight, gradient, first_moment, second, step_rate, decay_weight):
    first_new = beta_first * first_moment + (1.0 - beta_first) * gradient
    second_new = beta_second * second + (1.0 - beta_second) * gradient * gradient
    first_hat = first_new / (1.0 - beta_first**ADAM_STEP)
    second_hat = second_new / (1.0 - beta_second**ADAM_STEP)
    weight_new = weight - step_rate * (
        first_hat / (jnp.sqrt(second_hat) + adam_eps) + decay_weight * weight
    )
    return (weight_new, first_new, second_new)


def dot(left_array, right_array, left_dim, right_dim):
    return lax.dot_general(
        left_array,
        right_array,
        (((left_dim,), (right_dim,)), ((), ())),
        preferred_element_type=f32,
    )


def split_dot(left_f32, right_low, left_dim, right_dim):
    high = left_f32.astype(bf16)
    rest = left_f32 - high.astype(f32)
    low = rest.astype(bf16)
    return dot(high, right_low, left_dim, right_dim) + dot(low, right_low, left_dim, right_dim)


class Plan:
    def __init__(self, mesh):
        self.seqs = mesh.shape["fsdp"]
        self.ctx = mesh.shape["ctx"]
        self.total = self.ctx * self.seqs
        self.depth = DEPTH_PARTS
        self.across = self.ctx // self.depth
        self.plane = self.across * self.seqs
        self.core = self.seqs
        self.deep = [self.plane * step for step in range(1, self.depth)]
        bits = [1 << bit for bit in range(self.plane.bit_length() - 1)]
        self.flat = [bit for bit in bits if bit != self.core]
        self.near = [bit for bit in self.flat if bit > self.core]

    def swap(self, block, mask):
        return lax.ppermute(block, AXES, [(i, i ^ mask) for i in range(self.total)])


def join(plan, block, mask, kind):
    return kind.concatenate([block, plan.swap(block, mask)], 0)


def gather_flat(plan, block, kind=jnp, wait=None):
    half = block.shape[1] // 2
    first, last = block[None, :, :half], block[None, :, half:]
    for one, other in zip(plan.flat, plan.flat[::-1]):
        first, last = join(plan, first, one, kind), join(plan, last, other, kind)
    both = kind.stack([first, last])
    if wait is not None:
        both, wait = together(both, wait)
        return (both, plan.swap(both, plan.core)), wait
    return both, plan.swap(both, plan.core)


def keep_half(plan, block, mask):
    half = block.shape[0] // 2
    arrived = plan.swap(block[half:], mask)
    return (block[:half].astype(f32) + arrived.astype(f32)).astype(bf16)


def add_arrived(plan, kept, sent):
    return (kept.astype(f32) + plan.swap(sent, plan.core).astype(f32)).astype(bf16)


def scatter_flat(plan, blocks):
    return scatter_halves(plan, add_arrived(plan, *blocks))


def scatter_halves(plan, both):
    first, last = both[0], both[1]
    for one, other in zip(plan.flat[::-1], plan.flat):
        first, last = keep_half(plan, first, one), keep_half(plan, last, other)
    return jnp.concatenate([first[0], last[0]], 1)


def gather_deep(plan, block, kind=jnp):
    return kind.stack([block] + [plan.swap(block, mask) for mask in plan.deep])


def scatter_deep(plan, blocks):
    total = blocks[0].astype(f32)
    for step, mask in enumerate(plan.deep):
        total = total + plan.swap(blocks[step + 1], mask).astype(f32)
    return total


def spread_flat(plan, block):
    blocks = jnp.broadcast_to(block[None], (plan.plane,) + block.shape)
    return lax.all_to_all(blocks, ("t", "f"), split_axis=0, concat_axis=0, tiled=True)


def collect_flat(blocks):
    arrived = lax.all_to_all(blocks, ("t", "f"), split_axis=0, concat_axis=0, tiled=True)
    return jnp.sum(arrived.astype(f32), 0)


def together(*values):
    return lax.optimization_barrier(values)


class Traced(Plan):
    def swap(self, block, mask):
        moved = block.copy()
        moved[..., 0] ^= mask
        return moved


def row_sources(mesh, rows):
    start = np.zeros((rows, 2), np.int32)
    start[:, 1] = np.arange(rows)
    traced = Traced(mesh)
    return np.stack(gather_flat(traced, gather_deep(traced, start, np), np))


def key_sources(mesh):
    traced = Traced(mesh)
    deep = gather_deep(traced, np.zeros((1, 2), np.int32), np)
    return gather_keys(traced, deep, np)[:, 0, 0]


def token_sources(mesh):
    start = np.zeros((1, 2, 2), np.int32)
    start[:, :, 1] = np.arange(2)
    return np.stack(gather_flat(Traced(mesh), start, np)).reshape(-1, 2)


def gather_keys(plan, block, kind=jnp):
    block = block[None]
    for mask in plan.near:
        block = join(plan, block, mask, kind)
    block = join(plan, block[None], plan.core, kind)
    return block.reshape((-1,) + block.shape[-2:])


def scatter_keys(plan, blocks):
    order = (plan.across // 2, plan.depth, -1, blocks.shape[-1])
    blocks = blocks.reshape(order)
    for mask in plan.near[::-1]:
        blocks = keep_half(plan, blocks, mask)
    return scatter_deep(plan, blocks[0])


def rms(rows_f32):
    inverse = lax.rsqrt(jnp.mean(rows_f32 * rows_f32, -1, keepdims=True) + norm_eps)
    return inverse, rows_f32 * inverse


def turn(values, cosine, sine, sign):
    tile = 128
    lane = lax.broadcasted_iota(jnp.int32, (values.shape[0], tile), 1) % HEAD_DIM
    early = lane < HEAD_DIM // 2
    parts = []
    for start in range(0, values.shape[1], tile):
        part = values[:, start : start + tile]
        ahead = pltpu.roll(part, tile - HEAD_DIM // 2, 1)
        behind = pltpu.roll(part, HEAD_DIM // 2, 1)
        turned = jnp.where(early, -sign * ahead, sign * behind)
        parts.append(part * cosine + turned * sine)
    return jnp.concatenate(parts, 1) if len(parts) > 1 else parts[0]


def owned_by(owner, width, length):
    column = lax.broadcasted_iota(jnp.int32, (owner.shape[0], width), 1)
    return (column >= owner * length) & (column < (owner + 1) * length)


def lane_of(width, length, offset, lanes):
    entry = lax.broadcasted_iota(jnp.int32, (width, lanes), 0) % length
    lane = lax.broadcasted_iota(jnp.int32, (width, lanes), 1)
    return (lane == entry + offset).astype(bf16)


def times(left, first, last, lanes):
    half = first.shape[0]
    return dot(left[:, :half], first[:, lanes], 1, 0) + dot(left[:, half:], last[:, lanes], 1, 0)


def times_over(left, first, last, lanes):
    return jnp.concatenate(
        [dot(left, first[:, lanes], 1, 1), dot(left, last[:, lanes], 1, 1)], 1
    )


def project_kernel(
    sizes, rows, spread, marks, owner, pairs, first, last, cosine, sine,
    normed_out, query, key, value, gain_out, mlp_gain_out, place,
):
    lanes = slice(0, LANES)
    half = first.shape[0]
    spare = dot(marks[:half, :], first[:, lanes], 0, 0) + dot(marks[half:, :], last[:, lanes], 0, 0)
    spare = spare.astype(bf16)
    numbers = dot(pairs[...], spare, 1, 0)
    block = lax.broadcasted_iota(jnp.int32, (pairs.shape[0], place.shape[1]), 1).astype(f32)
    device = lax.broadcasted_iota(jnp.int32, block.shape, 0)
    offset = sum(length for length, width in sizes)
    where = jnp.zeros(block.shape, jnp.int32)
    for half_at in range(2):
        number = numbers[:, offset + half_at : offset + half_at + 1]
        where = where + jnp.where(number == block, 2 * device + half_at, 0)
    place[...] = jnp.sum(where, 0, keepdims=True)
    vectors, offset = [], 0
    for length, width in sizes:
        placed = dot(spare, lane_of(width, length, offset, LANES), 1, 1)
        mine = owned_by(owner[...], width, length)
        vectors.append(jnp.sum(jnp.where(mine, placed, 0.0), 0, keepdims=True))
        offset = offset + length
    gain, query_bias, value_bias, mlp_gain = vectors
    gain_out[...] = gain
    mlp_gain_out[...] = mlp_gain
    unused, unit = rms(rows[...].astype(f32))
    normed = (unit * gain).astype(bf16)
    placed = dot(normed, spread[...], 1, 0).astype(bf16)
    normed_out[...] = placed
    raw = times(placed, first, last, slice(0, WIDTH + 2 * KEY_WIDTH))
    cos, sin = cosine[...], sine[...]
    query[...] = turn(raw[:, :WIDTH] + query_bias, cos, sin, 1.0).astype(bf16)
    key[...] = turn(raw[:, WIDTH : WIDTH + KEY_WIDTH], cos, sin, 1.0).astype(bf16)
    value[...] = (raw[:, WIDTH + KEY_WIDTH :] + value_bias).astype(bf16)


def heads_of(ref, block, group, size):
    rows = pl.ds(block * size, size)
    first = group * GROUP * HEAD_DIM
    return jnp.concatenate(
        [ref[rows, first + h * HEAD_DIM : first + (h + 1) * HEAD_DIM] for h in range(GROUP)], 0
    )


def put_heads(ref, block, group, size, values):
    first = group * GROUP * HEAD_DIM
    for h in range(GROUP):
        ref[block * size : (block + 1) * size, first + h * HEAD_DIM : first + (h + 1) * HEAD_DIM] = (
            values[h * size : (h + 1) * size].astype(ref.dtype)
        )


def sort_keys(place, source, keys, values, size):
    def move(block, carry):
        start = pl.multiple_of(place[0, block] * size, size)
        target = pl.ds(pl.multiple_of(block * size, size), size)
        keys[target, :] = source[pl.ds(start, size), :KEY_WIDTH]
        values[target, :] = source[pl.ds(start, size), KEY_WIDTH:]
        return carry

    lax.fori_loop(0, keys.shape[0] // size, move, 0)


def turn_over(source, target, chunk):
    def move(step, carry):
        start = pl.multiple_of(step * chunk, chunk)
        part = source[pl.ds(start, chunk), :].astype(f32)
        target[:, pl.ds(start, chunk)] = part.T.astype(bf16)
        return carry

    lax.fori_loop(0, source.shape[0] // chunk, move, 0)


def masked(scores, start, block_at, size):
    key_pos = start + lax.broadcasted_iota(jnp.int32, scores.shape, 0)
    query_pos = block_at * size + lax.broadcasted_iota(jnp.int32, scores.shape, 1) % size
    return jnp.where(key_pos <= query_pos, scores, masked_score)


def over_chunks(step, block_at, size, chunk, carry):
    whole = (block_at * size) // chunk
    carry = lax.fori_loop(0, whole, functools.partial(step, False), carry)
    return step(True, whole, carry)


def scaled_heads(ref, block, group, size):
    return heads_of(ref, block, group, size) * bf16(HEAD_DIM ** (-0.5))


def attend_kernel(
    size, chunk, place, mine, query, keys, attended, log_total,
    sorted_keys, sorted_values, values_over,
):
    sort_keys(place, keys, sorted_keys, sorted_values, size)
    turn_over(sorted_values, values_over, chunk)
    columns = GROUP * size
    for block in range(2):
        block_at = mine[0, block * size] // size
        queries = [scaled_heads(query, block, group, size) for group in range(KV_HEADS)]

        def step(last, index, carry):
            start = pl.multiple_of(index * chunk, chunk)
            result = []
            for group in range(KV_HEADS):
                top, total, accum = carry[group]
                lanes = slice(group * HEAD_DIM, (group + 1) * HEAD_DIM)
                scores = dot(sorted_keys[pl.ds(start, chunk), lanes], queries[group], 1, 1)
                if last:
                    scores = masked(scores, start, block_at, size)
                new_top = jnp.maximum(top, jnp.max(scores, 0, keepdims=True))
                weights = jnp.exp(scores - new_top)
                scale = jnp.exp(top - new_top)
                total = total * scale + jnp.sum(weights, 0, keepdims=True)
                part = dot(values_over[lanes, pl.ds(start, chunk)], weights.astype(bf16), 1, 0)
                result.append((new_top, total, accum * scale + part))
            return tuple(result)

        zero = (
            jnp.full((1, columns), masked_score, f32),
            jnp.zeros((1, columns), f32),
            jnp.zeros((HEAD_DIM, columns), f32),
        )
        carry = over_chunks(step, block_at, size, chunk, (zero,) * KV_HEADS)
        for group in range(KV_HEADS):
            top, total, accum = carry[group]
            put_heads(attended, block, group, size, (accum / total).T)
            row = block * KV_HEADS + group
            log_total[row : row + 1, :] = top + jnp.log(total)


def backward_kernel(
    size, chunk, place, mine, query, keys, attended, attended_grad, log_total,
    query_grad, kept_grad, sent_grad,
    sorted_keys, sorted_values, keys_over, key_sums, value_sums,
):
    sort_keys(place, keys, sorted_keys, sorted_values, size)
    turn_over(sorted_keys, keys_over, chunk)
    key_sums[...] = jnp.zeros_like(key_sums)
    value_sums[...] = jnp.zeros_like(value_sums)
    columns = GROUP * size
    for block in range(2):
        block_at = mine[0, block * size] // size
        queries, grads, deltas, logs = [], [], [], []
        for group in range(KV_HEADS):
            queries.append(scaled_heads(query, block, group, size))
            grad = heads_of(attended_grad, block, group, size)
            out = heads_of(attended, block, group, size)
            grads.append(grad)
            deltas.append(
                jnp.sum((grad.astype(f32) * out.astype(f32)).T, 0, keepdims=True)
            )
            row = block * KV_HEADS + group
            logs.append(log_total[row : row + 1, :])

        def step(last, index, carry):
            start = pl.multiple_of(index * chunk, chunk)
            result = []
            for group in range(KV_HEADS):
                lanes = slice(group * HEAD_DIM, (group + 1) * HEAD_DIM)
                rows = pl.ds(start, chunk)
                scores = dot(sorted_keys[rows, lanes], queries[group], 1, 1)
                if last:
                    scores = masked(scores, start, block_at, size)
                probs = jnp.exp(scores - logs[group])
                prob_grad = dot(sorted_values[rows, lanes], grads[group], 1, 1)
                score_grad = (probs * (prob_grad - deltas[group])).astype(bf16)
                key_sums[group, rows, :] += dot(score_grad, queries[group], 1, 0)
                value_sums[group, rows, :] += dot(probs.astype(bf16), grads[group], 1, 0)
                result.append(carry[group] + dot(keys_over[lanes, rows], score_grad, 1, 0))
            return tuple(result)

        zero = jnp.zeros((HEAD_DIM, columns), f32)
        carry = over_chunks(step, block_at, size, chunk, (zero,) * KV_HEADS)
        for group in range(KV_HEADS):
            put_heads(query_grad, block, group, size, carry[group].T * HEAD_DIM ** (-0.5))

    span = kept_grad.shape[0] // size

    def move(block, carry):
        where = place[0, block]
        target = pl.ds(pl.multiple_of((where % span) * size, size), size)
        source = pl.ds(pl.multiple_of(block * size, size), size)
        total = jnp.concatenate(
            [sums[g, source, :] for sums in (key_sums, value_sums) for g in range(KV_HEADS)], 1
        ).astype(bf16)

        @pl.when(where < span)
        def keep():
            kept_grad[target, :] = total

        @pl.when(where >= span)
        def send():
            sent_grad[target, :] = total

        return carry

    lax.fori_loop(0, 2 * span, move, 0)


def pack_kernel(
    size, positions, query, keyval, output, norm_gain, query_bias, value_bias, mlp_gain, packed
):
    rows, width = query.shape
    side = keyval.shape[1]
    empty = packed.shape[0] - rows
    numbers = [
        jnp.full((1, 1), positions[0, half * size] // size, jnp.int32).astype(f32)
        for half in range(2)
    ]
    parts = [ref[...] for ref in (norm_gain, query_bias, value_bias, mlp_gain)] + numbers
    used = sum(part.shape[1] for part in parts)
    spare = jnp.concatenate(parts + [jnp.zeros((1, width - used), f32)], 1)
    packed[:, :width] = jnp.concatenate(
        [query[...], jnp.broadcast_to(spare, (empty, width))], 0
    ).astype(bf16)
    packed[:, width : width + side] = jnp.concatenate(
        [keyval[...], jnp.zeros((empty, side), f32)], 0
    ).astype(bf16)
    packed[:, width + side :] = jnp.concatenate(
        [output[...], jnp.zeros((empty, output.shape[1]), f32)], 0
    ).astype(bf16)


def slice_kernel(hidden, gate, up, sliced):
    plane, rows, width = sliced.shape
    half = width // 2
    depth = gate.shape[1] // (plane * hidden)
    for at, weight in enumerate((gate, up)):
        for t in range(plane):
            parts = [
                weight[:, (z * plane + t) * hidden : (z * plane + t + 1) * hidden]
                for z in range(depth)
            ]
            if half > depth * hidden:
                parts.append(jnp.zeros((rows, half - depth * hidden), f32))
            sliced[t, :, at * half : (at + 1) * half] = jnp.concatenate(parts, 1).astype(bf16)


def feed_kernel(
    size, group, places, first, last, cotangent, gate_up, down_rows,
    kept_grad, sent_grad, layer_terms, activated_out, hidden_grad, down,
):
    width = down.shape[0]
    spare = jnp.zeros((width - down_rows.shape[0], down.shape[1]), bf16)
    down[...] = jnp.concatenate([down_rows[...], spare], 0)
    halves = ((first, kept_grad), (last, sent_grad))
    count = first.shape[0] // (group * size)

    def step(side, index, carry):
        normed, normed_grad = halves[side]
        rows = pl.ds(pl.multiple_of(index * group * size, size), group * size)
        at = side * count + index
        all_rows = pl.ds(pl.multiple_of(at * group * size, size), group * size)
        spots = [
            pl.ds(pl.multiple_of(places[at * group + part] * size, size), size)
            for part in range(group)
        ]
        tokens = normed[rows, :]
        outs = jnp.concatenate([cotangent[spot, :] for spot in spots], 0)
        gate = dot(tokens, gate_up[:, :width], 1, 0)
        upper = dot(tokens, gate_up[:, width:], 1, 0)
        activated_grad = dot(outs, down[...], 1, 1)
        sigmoid = 1.0 / (1.0 + jnp.exp(-gate))
        silu = gate * sigmoid
        activated = (silu * upper).astype(bf16)
        gate_grad = (activated_grad * upper * sigmoid * (1.0 + gate * (1.0 - sigmoid))).astype(bf16)
        upper_grad = (activated_grad * silu).astype(bf16)
        hidden_grad[all_rows, :width] = gate_grad
        hidden_grad[all_rows, width:] = upper_grad
        normed_grad[rows, :] = (
            dot(gate_grad, gate_up[:, :width], 1, 1) + dot(upper_grad, gate_up[:, width:], 1, 1)
        ).astype(bf16)
        terms = dot(activated, down[...], 1, 0).astype(bf16)
        for part, spot in enumerate(spots):
            layer_terms[spot, :] = terms[part * size : (part + 1) * size]
            activated_out[spot, :] = activated[part * size : (part + 1) * size]
        return carry

    for side in range(2):
        lax.fori_loop(0, count, functools.partial(step, side), 0)


def mix_kernel(attended, spread, first, last, rows, gain, placed_out, mixed_out, normed_out):
    placed = dot(attended[...], spread[...], 1, 0).astype(bf16)
    placed_out[...] = placed
    mixed = rows[...].astype(f32) + times(placed, first, last, slice(0, WIDTH))
    mixed_out[...] = mixed
    unused, unit = rms(mixed)
    normed_out[...] = (unit * gain[...]).astype(bf16)


def rms_backward(residual, normed_grad, inverse, unit, gain):
    scaled = normed_grad * gain
    return residual + inverse * (scaled - unit * jnp.mean(scaled * unit, -1, keepdims=True))


def unmix_kernel(
    normed_grad, mixed, cotangent, gain, spread, first, last,
    mixed_grad_out, mixed_low_out, attended_grad, gain_grad,
):
    inverse, unit = rms(mixed[...])
    grad = normed_grad[...].astype(f32)
    gain_grad[...] = jnp.sum(grad * unit, 0, keepdims=True)
    mixed_grad = rms_backward(cotangent[...].astype(f32), grad, inverse, unit, gain[...])
    mixed_grad_out[...] = mixed_grad
    mixed_low = mixed_grad.astype(bf16)
    mixed_low_out[...] = mixed_low
    placed = times_over(mixed_low, first, last, slice(0, WIDTH)).astype(bf16)
    attended_grad[...] = dot(placed, spread[...], 1, 1).astype(bf16)


def finish_kernel(
    sizes, query_grad, key_grad, cosine, sine, rows, gain, spread, marks, owner, first, last,
    placed_normed, mixed_grad, mlp_gain_grad,
    input_grad, part_first, part_last,
):
    cos, sin = cosine[...], sine[...]
    dquery = turn(query_grad[...], cos, sin, -1.0)
    dkey = turn(key_grad[:, :KEY_WIDTH], cos, sin, -1.0)
    dvalue = key_grad[:, KEY_WIDTH:]
    low = jnp.concatenate([dquery, dkey, dvalue], 1).astype(bf16)
    normed_grad = split_dot(
        times_over(low, first, last, slice(0, WIDTH + 2 * KEY_WIDTH)), spread[...], 1, 1
    )
    inverse, unit = rms(rows[...].astype(f32))
    input_grad[...] = rms_backward(mixed_grad[...], normed_grad, inverse, unit, gain[...])
    vectors = (
        jnp.sum(normed_grad * unit, 0, keepdims=True),
        jnp.sum(dquery, 0, keepdims=True),
        jnp.sum(dvalue, 0, keepdims=True),
        mlp_gain_grad[...],
    )
    spare, offset = jnp.zeros((owner.shape[0], LANES), f32), 0
    for (length, width), vector in zip(sizes, vectors):
        mine = jnp.where(owned_by(owner[...], width, length), vector, 0.0)
        spare = spare + split_dot(mine, lane_of(width, length, offset, LANES), 1, 0)
        offset = offset + length
    half = first.shape[0]
    over = placed_normed[...].astype(f32).T.astype(bf16)
    for at, out in ((0, part_first), (half, part_last)):
        part = dot(over[at : at + half], low, 1, 0)
        out[:, :LANES] = (
            part[:, :LANES] + dot(marks[at : at + half, :], spare.astype(bf16), 1, 0)
        ).astype(bf16)
        out[:, LANES:] = part[:, LANES:].astype(bf16)


def update_kernel(hidden, sums, *refs):
    plane, rows, width = sums.shape
    half = width // 2
    depth = refs[0].shape[1] // (plane * hidden)
    for at in range(2):
        weight, first, second = refs[3 * at : 3 * at + 3]
        gradient, weight_new, first_new, second_new = refs[6 + 4 * at : 10 + 4 * at]
        for z in range(depth):
            for t in range(plane):
                start = (z * plane + t) * hidden
                source = at * half + z * hidden
                gradient[:, start : start + hidden] = sums[t, :, source : source + hidden].astype(f32)
        weight_new[...], first_new[...], second_new[...] = adamw_update(
            weight[...], gradient[...], first[...], second[...], matrix_rate, decay_rate
        )


def call(kernel, outs, scratch=(), scalars=0, name=None, cost=1):
    return pl.pallas_call(
        kernel,
        out_shape=[jax.ShapeDtypeStruct(shape, kind) for shape, kind in outs],
        in_specs=None if scalars is None else scalars,
        out_specs=[VMEM] * len(outs),
        scratch_shapes=list(scratch),
        compiler_params=pltpu.CompilerParams(vmem_limit_bytes=56 * 1024 * 1024),
        cost_estimate=pl.CostEstimate(
            flops=cost * 1_000_000_000, bytes_accessed=cost * 3_000_000, transcendentals=0
        ),
        name=name,
    )


def per_device(plan, mesh_sources, token_sources_of, key_masks, *arguments):
    layer_input, positions, out_grad = arguments[:3]
    masters, first_moments, second_moments = arguments[3:13], arguments[13:23], arguments[23:33]
    (
        norm_gain, query_proj, query_bias, keyval_proj, value_bias,
        output_proj, mlp_gain, gate_proj, up_proj, down_proj,
    ) = masters
    depth, plane, total = plan.depth, plan.plane, plan.total
    own = lax.axis_index(AXES)
    token_rows, position_rows, cotangent = layer_input[0], positions[0], out_grad[0]
    token_count = token_rows.shape[0]
    size = token_count // 2
    rows = query_proj.shape[0]
    vectors = (norm_gain, query_bias, value_bias, mlp_gain)
    vector_sizes = [vector.shape[0] for vector in vectors]
    vector_total = sum(vector_sizes)
    padded = -(-(rows + 1) // 16) * 16
    half = padded // 2
    qkv_width = query_proj.shape[1] + keyval_proj.shape[1]
    sources = mesh_sources(padded)
    flat_sources = sources.reshape(-1, 2)
    order = sources.shape[:-2]
    vector_masks = flat_sources[flat_sources[:, 1] == rows, 0]

    (block,) = call(
        functools.partial(pack_kernel, size),
        [((padded, qkv_width + WIDTH), bf16)],
        scalars=[SMEM] + [VMEM] * 7,
        name="pack",
        cost=2,
    )(positions, query_proj, keyval_proj, output_proj, *[vector[None] for vector in vectors])
    gate_shard, up_shard, block = together(gate_proj, up_proj, block)
    deep_blocks = gather_deep(plan, block)
    owner = own ^ jnp.asarray(flat_sources[:, 0])
    target = jnp.where(
        jnp.asarray(flat_sources[:, 1] < rows), owner * rows + jnp.asarray(flat_sources[:, 1]), -1
    )
    count = target.shape[0]
    column = lax.broadcasted_iota(jnp.int32, (WIDTH, count), 0)
    spread = (column == target[None]).astype(bf16)
    place_own = own % plane

    exponents = jnp.arange(HEAD_DIM // 2, dtype=f32) * (-2.0 / HEAD_DIM)
    inverse_freq = jnp.tile(jnp.power(f32(rope_base), exponents), 4)
    angles = position_rows.astype(f32)[:, None] * inverse_freq[None, :]
    cosine, sine = jnp.cos(angles), jnp.sin(angles)

    hidden = down_proj.shape[0]
    slice_width = hidden * depth
    slice_padded = -(-slice_width // 128) * 128

    (gate_up_parts,) = call(
        functools.partial(slice_kernel, hidden),
        [((plane, rows, 2 * slice_padded), bf16)],
        scalars=[VMEM] * 2,
        name="slices",
        cost=2,
    )(gate_shard, up_shard)
    gate_up_rows = lax.all_to_all(gate_up_parts, ("t", "f"), split_axis=0, concat_axis=0, tiled=True)
    down_low = lax.all_gather(down_proj.astype(bf16), "z", axis=0, tiled=True)
    deep_blocks, gate_up_rows, spread, cosine, sine = together(
        deep_blocks, gate_up_rows, spread, cosine, sine
    )
    gate_up_low = lax.all_gather(
        gate_up_rows.reshape(plane * rows, 2 * slice_padded), "z", axis=0, tiled=True
    )
    weights = [
        blocks.reshape(-1, qkv_width)
        for blocks in gather_flat(plan, deep_blocks[:, :, :qkv_width])
    ]
    vector_owner = (own ^ jnp.asarray(vector_masks))[:, None]
    vector_at = flat_sources[:, 1] == rows
    marks = jnp.asarray(
        (np.flatnonzero(vector_at)[None] == np.arange(len(vector_at))[:, None]).astype(np.float32)
    ).astype(bf16)
    pairs = jnp.asarray((key_masks[:, None] == vector_masks[None]).astype(np.float32)).astype(bf16)
    sizes = [(length, length * total) for length in vector_sizes]

    placed_normed, query_rot, key_rot, value_low, gain_row, mlp_gain_row, place = call(
        functools.partial(project_kernel, sizes),
        [
            ((token_count, count), bf16),
            ((token_count, WIDTH), bf16),
            ((token_count, KEY_WIDTH), bf16),
            ((token_count, KEY_WIDTH), bf16),
            ((1, WIDTH), f32),
            ((1, WIDTH), f32),
            ((1, -(-2 * plan.ctx // LANES) * LANES), jnp.int32),
        ],
        scalars=[VMEM] * 9,
        name="project",
    )(token_rows, spread, marks, vector_owner, pairs, *weights, cosine, sine)

    output_blocks, key_rot = together(deep_blocks[:, :, qkv_width:], key_rot)
    deep_keys = gather_deep(plan, jnp.concatenate([key_rot, value_low], 1))
    output_weights = [blocks.reshape(-1, WIDTH) for blocks in gather_flat(plan, output_blocks)]
    all_keys = gather_keys(plan, deep_keys)
    cotangent, all_keys, output_weights = together(cotangent, all_keys, output_weights)
    all_cotangent = spread_flat(plan, cotangent).reshape(-1, WIDTH)
    key_rows = all_keys.shape[0] * token_count
    all_keys = all_keys.reshape(-1, 2 * KEY_WIDTH)
    chunk = KEY_CHUNK
    attended, log_total = call(
        functools.partial(attend_kernel, size, chunk),
        [((token_count, WIDTH), bf16), ((2 * KV_HEADS, GROUP * size), f32)],
        scratch=[
            pltpu.VMEM((key_rows, KEY_WIDTH), bf16),
            pltpu.VMEM((key_rows, KEY_WIDTH), bf16),
            pltpu.VMEM((KEY_WIDTH, key_rows), bf16),
        ],
        scalars=[SMEM, SMEM] + [VMEM] * 2,
        name="attend",
    )(place, positions, query_rot, all_keys)

    attended, gate_up_low = together(attended, gate_up_low)
    placed_attended, mixed, normed_mixed = call(
        mix_kernel,
        [
            ((token_count, count), bf16),
            ((token_count, WIDTH), f32),
            ((token_count, WIDTH), bf16),
        ],
        scalars=[VMEM] * 6,
        name="mix",
    )(attended, spread, *output_weights, token_rows, mlp_gain_row)

    normed_mixed, all_cotangent = together(normed_mixed, all_cotangent)
    normed_blocks, down_low = gather_flat(plan, normed_mixed[None], wait=down_low)
    token_order = normed_blocks[0].shape
    normed_blocks = [blocks.reshape(-1, WIDTH) for blocks in normed_blocks]
    token_total = 2 * normed_blocks[0].shape[0]
    moves = jnp.asarray(token_sources_of)
    places = (place_own ^ moves[:, 0]) * 2 + moves[:, 1]
    kept_terms, sent_terms, layer_terms, activated, hidden_grad = call(
        functools.partial(feed_kernel, size, 8),
        [
            ((token_total // 2, WIDTH), bf16),
            ((token_total // 2, WIDTH), bf16),
            ((token_total, WIDTH), bf16),
            ((token_total, slice_padded), bf16),
            ((token_total, 2 * slice_padded), bf16),
        ],
        scratch=[pltpu.VMEM((slice_padded, WIDTH), bf16)],
        scalars=[SMEM] + [VMEM] * 5,
        name="feed",
        cost=16,
    )(places, *normed_blocks, all_cotangent, gate_up_low, down_low)
    kept_terms = add_arrived(
        plan, kept_terms.reshape(token_order), sent_terms.reshape(token_order)
    )
    hidden_grad, kept_terms = together(hidden_grad, kept_terms)
    split = token_total // 2
    part_gate_up = (
        dot(normed_blocks[0], hidden_grad[:split], 0, 0)
        + dot(normed_blocks[1], hidden_grad[split:], 0, 0)
    ).astype(bf16)
    normed_mixed_grad = scatter_halves(plan, kept_terms)[0]
    layer_terms, normed_mixed_grad = together(layer_terms, normed_mixed_grad)

    mixed_grad, mixed_low, attended_grad, part_mgain = call(
        unmix_kernel,
        [
            ((token_count, WIDTH), f32),
            ((token_count, WIDTH), bf16),
            ((token_count, WIDTH), bf16),
            ((1, WIDTH), f32),
        ],
        scalars=[VMEM] * 7,
        name="unmix",
        cost=5,
    )(normed_mixed_grad, mixed, cotangent, mlp_gain_row, spread, *output_weights)

    gate_up_sum = lax.psum_scatter(part_gate_up, "z", scatter_dimension=0, tiled=True)
    layer_terms = layer_terms.reshape(plane, token_count, WIDTH)
    layer_terms = lax.all_to_all(layer_terms, ("t", "f"), split_axis=0, concat_axis=0, tiled=True)

    part_output = dot(placed_attended, mixed_low, 0, 0).astype(bf16)
    part_output = part_output.reshape(order + (half, WIDTH))
    part_output = add_arrived(plan, part_output[0], part_output[1])
    query_rot_grad, *key_terms = call(
        functools.partial(backward_kernel, size, chunk),
        [
            ((token_count, WIDTH), f32),
            ((key_rows // 2, 2 * KEY_WIDTH), bf16),
            ((key_rows // 2, 2 * KEY_WIDTH), bf16),
        ],
        scratch=[
            pltpu.VMEM((key_rows, KEY_WIDTH), bf16),
            pltpu.VMEM((key_rows, KEY_WIDTH), bf16),
            pltpu.VMEM((KEY_WIDTH, key_rows), bf16),
            pltpu.VMEM((KV_HEADS, key_rows, HEAD_DIM), f32),
            pltpu.VMEM((KV_HEADS, key_rows, HEAD_DIM), f32),
        ],
        scalars=[SMEM, SMEM] + [VMEM] * 5,
        name="backward",
        cost=16,
    )(place, positions, query_rot, all_keys, attended, attended_grad, log_total)
    key_terms, layer_terms = together(key_terms, layer_terms)
    key_terms = add_arrived(plan, *key_terms)
    activated, key_terms = together(activated, key_terms)
    part_down = dot(activated, all_cotangent, 0, 0)[:slice_width].astype(bf16)
    part_down, gate_up_sum = together(part_down, gate_up_sum)
    down_sum = lax.psum_scatter(part_down, "z", scatter_dimension=0, tiled=True)
    key_sum = scatter_keys(plan, key_terms)

    gate_up_sum = lax.all_to_all(
        gate_up_sum.reshape(plane, rows, 2 * slice_padded),
        ("t", "f"), split_axis=0, concat_axis=0, tiled=True,
    )
    layer_rows = (mixed + jnp.sum(layer_terms.astype(f32), 0)).astype(bf16)
    input_rows, *part_qkv = call(
        functools.partial(finish_kernel, sizes),
        [
            ((token_count, WIDTH), f32),
            ((count // 2, qkv_width), bf16),
            ((count // 2, qkv_width), bf16),
        ],
        scalars=[VMEM] * 14,
        name="finish",
        cost=9,
    )(
        query_rot_grad, key_sum, cosine, sine, token_rows, gain_row, spread, marks, vector_owner,
        *weights, placed_normed, mixed_grad, part_mgain,
    )
    part_qkv = [part.reshape(order[1:] + (half, qkv_width)) for part in part_qkv]
    part_qkv, gate_up_sum = together(part_qkv, gate_up_sum)
    part_qkv = add_arrived(plan, *part_qkv)
    gate_up_sum, part_qkv = together(gate_up_sum, part_qkv)
    weight_sums = scatter_halves(plan, jnp.concatenate([part_qkv, part_output], -1))
    weight_sums = scatter_deep(plan, weight_sums)
    qkv_sum = weight_sums[:, :qkv_width]
    grad_output = weight_sums[:rows, qkv_width:]

    grad_gate, *new_gate, grad_up, new_up, new_up_mean, new_up_square = call(
        functools.partial(update_kernel, hidden),
        [(gate_proj.shape, f32)] * 8,
        scalars=[VMEM] * 7,
        name="update",
        cost=6,
    )(
        gate_up_sum, gate_proj, first_moments[7], second_moments[7],
        up_proj, first_moments[8], second_moments[8],
    )
    new_up = [new_up, new_up_mean, new_up_square]
    grad_down = down_sum.astype(f32)
    grad_query = qkv_sum[:rows, :WIDTH]
    grad_keyval = qkv_sum[:rows, WIDTH:]
    vector_sums = qkv_sum[rows]
    vector_grads = []
    offset = 0
    for length in vector_sizes:
        vector_grads.append(vector_sums[offset : offset + length])
        offset = offset + length
    grad_gain, grad_qbias, grad_vbias, grad_mgain = vector_grads
    gradients = (
        grad_gain, grad_query, grad_qbias, grad_keyval, grad_vbias,
        grad_output, grad_mgain, grad_gate, grad_up, grad_down,
    )
    vector, matrix = (vector_rate, 0.0), (matrix_rate, decay_rate)
    settings = (
        vector, matrix, vector, matrix, vector, (output_rate, decay_rate), vector,
        matrix, matrix, matrix,
    )
    updated = [
        adamw_update(weight, gradient, first_moment, second, setting[0], setting[1])
        for weight, gradient, first_moment, second, setting in zip(
            masters, gradients, first_moments, second_moments, settings
        )
    ]
    updated[7], updated[8] = new_gate, new_up
    return (
        (layer_rows[None], input_rows[None])
        + tuple(gradients)
        + tuple((entry[0] for entry in updated))
        + tuple((entry[1] for entry in updated))
        + tuple((entry[2] for entry in updated))
    )


def solution(mesh):
    plan = Plan(mesh)
    devices = mesh.devices.reshape(plan.depth, plan.across, plan.seqs)
    return jax.shard_map(
        functools.partial(
            per_device, plan, functools.partial(row_sources, mesh), token_sources(mesh),
            key_sources(mesh),
        ),
        mesh=Mesh(devices, AXES),
        in_specs=(
            P("f", ("z", "t"), None),
            P("f", ("z", "t")),
            P("f", ("z", "t"), None),
            P(AXES),
            P(AXES, None),
            P(AXES),
            P(AXES, None),
            P(AXES),
            P(AXES, None),
            P(AXES),
            P(AXES, None),
            P(AXES, None),
            P(AXES, None),
            P(AXES),
            P(AXES, None),
            P(AXES),
            P(AXES, None),
            P(AXES),
            P(AXES, None),
            P(AXES),
            P(AXES, None),
            P(AXES, None),
            P(AXES, None),
            P(AXES),
            P(AXES, None),
            P(AXES),
            P(AXES, None),
            P(AXES),
            P(AXES, None),
            P(AXES),
            P(AXES, None),
            P(AXES, None),
            P(AXES, None),
        ),
        out_specs=(
            P("f", ("z", "t"), None),
            P("f", ("z", "t"), None),
            P(AXES),
            P(AXES, None),
            P(AXES),
            P(AXES, None),
            P(AXES),
            P(AXES, None),
            P(AXES),
            P(AXES, None),
            P(AXES, None),
            P(AXES, None),
            P(AXES),
            P(AXES, None),
            P(AXES),
            P(AXES, None),
            P(AXES),
            P(AXES, None),
            P(AXES),
            P(AXES, None),
            P(AXES, None),
            P(AXES, None),
            P(AXES),
            P(AXES, None),
            P(AXES),
            P(AXES, None),
            P(AXES),
            P(AXES, None),
            P(AXES),
            P(AXES, None),
            P(AXES, None),
            P(AXES, None),
            P(AXES),
            P(AXES, None),
            P(AXES),
            P(AXES, None),
            P(AXES),
            P(AXES, None),
            P(AXES),
            P(AXES, None),
            P(AXES, None),
            P(AXES, None),
        ),
        check_vma=False,
    )
```

```python
import functools

import jax
import jax.numpy as jnp
import numpy as np
from jax import lax
from jax.experimental import pallas as pl
from jax.experimental.pallas import tpu as pltpu
from jax.sharding import Mesh
from jax.sharding import PartitionSpec as P

HEAD_DIM = 64
HEADS = 14
KV_HEADS = 2
ADAM_STEP = 4
GROUP = 7
KEY_WIDTH = KV_HEADS * HEAD_DIM
WIDTH = HEADS * HEAD_DIM


norm_eps = 1e-06
rope_base = 1000000.0
beta_first = 0.9
beta_second = 0.95
adam_eps = 1e-08
matrix_rate = 0.03
output_rate = 0.6
vector_rate = 0.5
decay_rate = 0.1
masked_score = -1e30
f32 = jnp.float32
bf16 = jnp.bfloat16
DEPTH_PARTS = 4
KEY_CHUNK = 512
LANES = 128
VMEM = pl.BlockSpec(memory_space=pltpu.VMEM)
SMEM = pl.BlockSpec(memory_space=pltpu.SMEM)
AXES = ("z", "t", "f")


def adamw_update(weight, gradient, first_moment, second, step_rate, decay_weight):
    first_new = beta_first * first_moment + (1.0 - beta_first) * gradient
    second_new = beta_second * second + (1.0 - beta_second) * gradient * gradient
    first_hat = first_new / (1.0 - beta_first**ADAM_STEP)
    second_hat = second_new / (1.0 - beta_second**ADAM_STEP)
    weight_new = weight - step_rate * (
        first_hat / (jnp.sqrt(second_hat) + adam_eps) + decay_weight * weight
    )
    return (weight_new, first_new, second_new)


def dot(left_array, right_array, left_dim, right_dim):
    return lax.dot_general(
        left_array,
        right_array,
        (((left_dim,), (right_dim,)), ((), ())),
        preferred_element_type=f32,
    )


def split_dot(left_f32, right_low, left_dim, right_dim):
    high = left_f32.astype(bf16)
    rest = left_f32 - high.astype(f32)
    low = rest.astype(bf16)
    return dot(high, right_low, left_dim, right_dim) + dot(low, right_low, left_dim, right_dim)


class Plan:
    def __init__(self, mesh):
        self.seqs = mesh.shape["fsdp"]
        self.ctx = mesh.shape["ctx"]
        self.total = self.ctx * self.seqs
        self.depth = DEPTH_PARTS
        self.across = self.ctx // self.depth
        self.plane = self.across * self.seqs
        self.core = self.seqs
        self.deep = [self.plane * step for step in range(1, self.depth)]
        bits = [1 << bit for bit in range(self.plane.bit_length() - 1)]
        self.flat = [bit for bit in bits if bit != self.core]
        self.near = [bit for bit in self.flat if bit > self.core]

    def swap(self, block, mask):
        return lax.ppermute(block, AXES, [(i, i ^ mask) for i in range(self.total)])


def join(plan, block, mask, kind):
    return kind.concatenate([block, plan.swap(block, mask)], 0)


def gather_flat(plan, block, kind=jnp, wait=None):
    half = block.shape[1] // 2
    first, last = block[None, :, :half], block[None, :, half:]
    for one, other in zip(plan.flat, plan.flat[::-1]):
        first, last = join(plan, first, one, kind), join(plan, last, other, kind)
    both = kind.stack([first, last])
    if wait is not None:
        both, wait = together(both, wait)
        return (both, plan.swap(both, plan.core)), wait
    return both, plan.swap(both, plan.core)


def keep_half(plan, block, mask):
    half = block.shape[0] // 2
    arrived = plan.swap(block[half:], mask)
    return (block[:half].astype(f32) + arrived.astype(f32)).astype(bf16)


def add_arrived(plan, kept, sent):
    return (kept.astype(f32) + plan.swap(sent, plan.core).astype(f32)).astype(bf16)


def scatter_flat(plan, blocks):
    return scatter_halves(plan, add_arrived(plan, *blocks))


def scatter_halves(plan, both, beside=None):
    first, last = both[0], both[1]
    for step, (one, other) in enumerate(zip(plan.flat[::-1], plan.flat)):
        first, last = keep_half(plan, first, one), keep_half(plan, last, other)
        if beside is not None and step == 0:
            first, last, *beside = together(first, last, *beside)
    blocks = jnp.concatenate([first[0], last[0]], 1)
    return blocks if beside is None else (blocks, beside)


def gather_deep(plan, block, kind=jnp):
    return kind.stack([block] + [plan.swap(block, mask) for mask in plan.deep])


def scatter_deep(plan, blocks):
    total = blocks[0].astype(f32)
    for step, mask in enumerate(plan.deep):
        total = total + plan.swap(blocks[step + 1], mask).astype(f32)
    return total


def spread_flat(plan, block):
    blocks = jnp.broadcast_to(block[None], (plan.plane,) + block.shape)
    return lax.all_to_all(blocks, ("t", "f"), split_axis=0, concat_axis=0, tiled=True)


def collect_flat(blocks):
    arrived = lax.all_to_all(blocks, ("t", "f"), split_axis=0, concat_axis=0, tiled=True)
    return jnp.sum(arrived.astype(f32), 0)


def together(*values):
    return lax.optimization_barrier(values)


class Traced(Plan):
    def swap(self, block, mask):
        moved = block.copy()
        moved[..., 0] ^= mask
        return moved


def row_sources(mesh, rows):
    start = np.zeros((rows, 2), np.int32)
    start[:, 1] = np.arange(rows)
    traced = Traced(mesh)
    return np.stack(gather_flat(traced, gather_deep(traced, start, np), np))


def key_sources(mesh):
    traced = Traced(mesh)
    deep = gather_deep(traced, np.zeros((1, 2), np.int32), np)
    return gather_keys(traced, deep, np)[:, 0, 0]


def token_sources(mesh):
    start = np.zeros((1, 2, 2), np.int32)
    start[:, :, 1] = np.arange(2)
    return np.stack(gather_flat(Traced(mesh), start, np)).reshape(-1, 2)


def gather_keys(plan, block, kind=jnp):
    block = block[None]
    for mask in plan.near:
        block = join(plan, block, mask, kind)
    block = join(plan, block[None], plan.core, kind)
    return block.reshape((-1,) + block.shape[-2:])


def scatter_keys(plan, blocks):
    order = (plan.across // 2, plan.depth, -1, blocks.shape[-1])
    blocks = blocks.reshape(order)
    for mask in plan.near[::-1]:
        blocks = keep_half(plan, blocks, mask)
    return scatter_deep(plan, blocks[0])


def rms(rows_f32):
    inverse = lax.rsqrt(jnp.mean(rows_f32 * rows_f32, -1, keepdims=True) + norm_eps)
    return inverse, rows_f32 * inverse


def turn(values, cosine, sine, sign):
    tile = 128
    lane = lax.broadcasted_iota(jnp.int32, (values.shape[0], tile), 1) % HEAD_DIM
    early = lane < HEAD_DIM // 2
    parts = []
    for start in range(0, values.shape[1], tile):
        part = values[:, start : start + tile]
        ahead = pltpu.roll(part, tile - HEAD_DIM // 2, 1)
        behind = pltpu.roll(part, HEAD_DIM // 2, 1)
        turned = jnp.where(early, -sign * ahead, sign * behind)
        parts.append(part * cosine + turned * sine)
    return jnp.concatenate(parts, 1) if len(parts) > 1 else parts[0]


def owned_by(owner, width, length):
    column = lax.broadcasted_iota(jnp.int32, (owner.shape[0], width), 1)
    return (column >= owner * length) & (column < (owner + 1) * length)


def lane_of(width, length, offset, lanes):
    entry = lax.broadcasted_iota(jnp.int32, (width, lanes), 0) % length
    lane = lax.broadcasted_iota(jnp.int32, (width, lanes), 1)
    return (lane == entry + offset).astype(bf16)


def times(left, first, last, lanes):
    half = first.shape[0]
    return dot(left[:, :half], first[:, lanes], 1, 0) + dot(left[:, half:], last[:, lanes], 1, 0)


def times_over(left, first, last, lanes):
    return jnp.concatenate(
        [dot(left, first[:, lanes], 1, 1), dot(left, last[:, lanes], 1, 1)], 1
    )


def project_kernel(
    sizes, rows, spread, marks, owner, pairs, first, last, cosine, sine,
    normed_out, query, key, value, gain_out, mlp_gain_out, place,
):
    lanes = slice(0, LANES)
    half = first.shape[0]
    spare = dot(marks[:half, :], first[:, lanes], 0, 0) + dot(marks[half:, :], last[:, lanes], 0, 0)
    spare = spare.astype(bf16)
    numbers = dot(pairs[...], spare, 1, 0)
    block = lax.broadcasted_iota(jnp.int32, (pairs.shape[0], place.shape[1]), 1).astype(f32)
    device = lax.broadcasted_iota(jnp.int32, block.shape, 0)
    offset = sum(length for length, width in sizes)
    where = jnp.zeros(block.shape, jnp.int32)
    for half_at in range(2):
        number = numbers[:, offset + half_at : offset + half_at + 1]
        where = where + jnp.where(number == block, 2 * device + half_at, 0)
    place[...] = jnp.sum(where, 0, keepdims=True)
    vectors, offset = [], 0
    for length, width in sizes:
        placed = dot(spare, lane_of(width, length, offset, LANES), 1, 1)
        mine = owned_by(owner[...], width, length)
        vectors.append(jnp.sum(jnp.where(mine, placed, 0.0), 0, keepdims=True))
        offset = offset + length
    gain, query_bias, value_bias, mlp_gain = vectors
    gain_out[...] = gain
    mlp_gain_out[...] = mlp_gain
    unused, unit = rms(rows[...].astype(f32))
    normed = (unit * gain).astype(bf16)
    placed = dot(normed, spread[...], 1, 0).astype(bf16)
    normed_out[...] = placed
    raw = times(placed, first, last, slice(0, WIDTH + 2 * KEY_WIDTH))
    cos, sin = cosine[...], sine[...]
    query[...] = turn(raw[:, :WIDTH] + query_bias, cos, sin, 1.0).astype(bf16)
    key[...] = turn(raw[:, WIDTH : WIDTH + KEY_WIDTH], cos, sin, 1.0).astype(bf16)
    value[...] = (raw[:, WIDTH + KEY_WIDTH :] + value_bias).astype(bf16)


def heads_of(ref, block, group, size):
    rows = pl.ds(block * size, size)
    first = group * GROUP * HEAD_DIM
    return jnp.concatenate(
        [ref[rows, first + h * HEAD_DIM : first + (h + 1) * HEAD_DIM] for h in range(GROUP)], 0
    )


def put_heads(ref, block, group, size, values):
    first = group * GROUP * HEAD_DIM
    for h in range(GROUP):
        ref[block * size : (block + 1) * size, first + h * HEAD_DIM : first + (h + 1) * HEAD_DIM] = (
            values[h * size : (h + 1) * size].astype(ref.dtype)
        )


def sort_keys(place, source, keys, values, size):
    def move(block, carry):
        start = pl.multiple_of(place[0, block] * size, size)
        target = pl.ds(pl.multiple_of(block * size, size), size)
        keys[target, :] = source[pl.ds(start, size), :KEY_WIDTH]
        values[target, :] = source[pl.ds(start, size), KEY_WIDTH:]
        return carry

    lax.fori_loop(0, keys.shape[0] // size, move, 0)


def turn_over(source, target, chunk):
    def move(step, carry):
        start = pl.multiple_of(step * chunk, chunk)
        part = source[pl.ds(start, chunk), :].astype(f32)
        target[:, pl.ds(start, chunk)] = part.T.astype(bf16)
        return carry

    lax.fori_loop(0, source.shape[0] // chunk, move, 0)


def masked(scores, start, block_at, size):
    key_pos = start + lax.broadcasted_iota(jnp.int32, scores.shape, 0)
    query_pos = block_at * size + lax.broadcasted_iota(jnp.int32, scores.shape, 1) % size
    return jnp.where(key_pos <= query_pos, scores, masked_score)


def over_chunks(step, block_at, size, chunk, carry):
    whole = (block_at * size) // chunk
    carry = lax.fori_loop(0, whole, functools.partial(step, False), carry)
    return step(True, whole, carry)


def scaled_heads(ref, block, group, size):
    return heads_of(ref, block, group, size) * bf16(HEAD_DIM ** (-0.5))


def attend_kernel(
    size, chunk, place, mine, query, keys, attended, log_total,
    sorted_keys, sorted_values, values_over,
):
    sort_keys(place, keys, sorted_keys, sorted_values, size)
    turn_over(sorted_values, values_over, chunk)
    columns = GROUP * size
    for block in range(2):
        block_at = mine[0, block * size] // size
        queries = [scaled_heads(query, block, group, size) for group in range(KV_HEADS)]

        def step(last, index, carry):
            start = pl.multiple_of(index * chunk, chunk)
            result = []
            for group in range(KV_HEADS):
                top, total, accum = carry[group]
                lanes = slice(group * HEAD_DIM, (group + 1) * HEAD_DIM)
                scores = dot(sorted_keys[pl.ds(start, chunk), lanes], queries[group], 1, 1)
                if last:
                    scores = masked(scores, start, block_at, size)
                new_top = jnp.maximum(top, jnp.max(scores, 0, keepdims=True))
                weights = jnp.exp(scores - new_top)
                scale = jnp.exp(top - new_top)
                total = total * scale + jnp.sum(weights, 0, keepdims=True)
                part = dot(values_over[lanes, pl.ds(start, chunk)], weights.astype(bf16), 1, 0)
                result.append((new_top, total, accum * scale + part))
            return tuple(result)

        zero = (
            jnp.full((1, columns), masked_score, f32),
            jnp.zeros((1, columns), f32),
            jnp.zeros((HEAD_DIM, columns), f32),
        )
        carry = over_chunks(step, block_at, size, chunk, (zero,) * KV_HEADS)
        for group in range(KV_HEADS):
            top, total, accum = carry[group]
            put_heads(attended, block, group, size, (accum / total).T)
            row = block * KV_HEADS + group
            log_total[row : row + 1, :] = top + jnp.log(total)


def backward_kernel(
    size, chunk, place, mine, query, keys, attended, attended_grad, log_total,
    query_grad, kept_grad, sent_grad,
    sorted_keys, sorted_values, keys_over, key_sums, value_sums,
):
    sort_keys(place, keys, sorted_keys, sorted_values, size)
    turn_over(sorted_keys, keys_over, chunk)
    key_sums[...] = jnp.zeros_like(key_sums)
    value_sums[...] = jnp.zeros_like(value_sums)
    columns = GROUP * size
    for block in range(2):
        block_at = mine[0, block * size] // size
        queries, grads, deltas, logs = [], [], [], []
        for group in range(KV_HEADS):
            queries.append(scaled_heads(query, block, group, size))
            grad = heads_of(attended_grad, block, group, size)
            out = heads_of(attended, block, group, size)
            grads.append(grad)
            deltas.append(
                jnp.sum((grad.astype(f32) * out.astype(f32)).T, 0, keepdims=True)
            )
            row = block * KV_HEADS + group
            logs.append(log_total[row : row + 1, :])

        def step(last, index, carry):
            start = pl.multiple_of(index * chunk, chunk)
            result = []
            for group in range(KV_HEADS):
                lanes = slice(group * HEAD_DIM, (group + 1) * HEAD_DIM)
                rows = pl.ds(start, chunk)
                scores = dot(sorted_keys[rows, lanes], queries[group], 1, 1)
                if last:
                    scores = masked(scores, start, block_at, size)
                probs = jnp.exp(scores - logs[group])
                prob_grad = dot(sorted_values[rows, lanes], grads[group], 1, 1)
                score_grad = (probs * (prob_grad - deltas[group])).astype(bf16)
                key_sums[group, rows, :] += dot(score_grad, queries[group], 1, 0)
                value_sums[group, rows, :] += dot(probs.astype(bf16), grads[group], 1, 0)
                result.append(carry[group] + dot(keys_over[lanes, rows], score_grad, 1, 0))
            return tuple(result)

        zero = jnp.zeros((HEAD_DIM, columns), f32)
        carry = over_chunks(step, block_at, size, chunk, (zero,) * KV_HEADS)
        for group in range(KV_HEADS):
            put_heads(query_grad, block, group, size, carry[group].T * HEAD_DIM ** (-0.5))

    span = kept_grad.shape[0] // size

    def move(block, carry):
        where = place[0, block]
        target = pl.ds(pl.multiple_of((where % span) * size, size), size)
        source = pl.ds(pl.multiple_of(block * size, size), size)
        total = jnp.concatenate(
            [sums[g, source, :] for sums in (key_sums, value_sums) for g in range(KV_HEADS)], 1
        ).astype(bf16)

        @pl.when(where < span)
        def keep():
            kept_grad[target, :] = total

        @pl.when(where >= span)
        def send():
            sent_grad[target, :] = total

        return carry

    lax.fori_loop(0, 2 * span, move, 0)


def pack_kernel(
    size, positions, query, keyval, output, norm_gain, query_bias, value_bias, mlp_gain, packed
):
    rows, width = query.shape
    side = keyval.shape[1]
    empty = packed.shape[0] - rows
    numbers = [
        jnp.full((1, 1), positions[0, half * size] // size, jnp.int32).astype(f32)
        for half in range(2)
    ]
    parts = [ref[...] for ref in (norm_gain, query_bias, value_bias, mlp_gain)] + numbers
    used = sum(part.shape[1] for part in parts)
    spare = jnp.concatenate(parts + [jnp.zeros((1, width - used), f32)], 1)
    packed[:, :width] = jnp.concatenate(
        [query[...], jnp.broadcast_to(spare, (empty, width))], 0
    ).astype(bf16)
    packed[:, width : width + side] = jnp.concatenate(
        [keyval[...], jnp.zeros((empty, side), f32)], 0
    ).astype(bf16)
    packed[:, width + side :] = jnp.concatenate(
        [output[...], jnp.zeros((empty, output.shape[1]), f32)], 0
    ).astype(bf16)


def slice_kernel(hidden, gate, up, sliced):
    plane, rows, width = sliced.shape
    half = width // 2
    depth = gate.shape[1] // (plane * hidden)
    for at, weight in enumerate((gate, up)):
        for t in range(plane):
            parts = [
                weight[:, (z * plane + t) * hidden : (z * plane + t + 1) * hidden]
                for z in range(depth)
            ]
            if half > depth * hidden:
                parts.append(jnp.zeros((rows, half - depth * hidden), f32))
            sliced[t, :, at * half : (at + 1) * half] = jnp.concatenate(parts, 1).astype(bf16)


def feed_kernel(
    size, group, places, first, last, cotangent, gate_up, down_rows,
    kept_grad, sent_grad, layer_terms, activated_out, hidden_grad, down,
):
    width = down.shape[0]
    spare = jnp.zeros((width - down_rows.shape[0], down.shape[1]), bf16)
    down[...] = jnp.concatenate([down_rows[...], spare], 0)
    halves = ((first, kept_grad), (last, sent_grad))
    count = first.shape[0] // (group * size)

    def step(side, index, carry):
        normed, normed_grad = halves[side]
        rows = pl.ds(pl.multiple_of(index * group * size, size), group * size)
        at = side * count + index
        all_rows = pl.ds(pl.multiple_of(at * group * size, size), group * size)
        spots = [
            pl.ds(pl.multiple_of(places[at * group + part] * size, size), size)
            for part in range(group)
        ]
        tokens = normed[rows, :]
        outs = jnp.concatenate([cotangent[spot, :] for spot in spots], 0)
        gate = dot(tokens, gate_up[:, :width], 1, 0)
        upper = dot(tokens, gate_up[:, width:], 1, 0)
        activated_grad = dot(outs, down[...], 1, 1)
        sigmoid = 1.0 / (1.0 + jnp.exp(-gate))
        silu = gate * sigmoid
        activated = (silu * upper).astype(bf16)
        gate_grad = (activated_grad * upper * sigmoid * (1.0 + gate * (1.0 - sigmoid))).astype(bf16)
        upper_grad = (activated_grad * silu).astype(bf16)
        hidden_grad[all_rows, :width] = gate_grad
        hidden_grad[all_rows, width:] = upper_grad
        normed_grad[rows, :] = (
            dot(gate_grad, gate_up[:, :width], 1, 1) + dot(upper_grad, gate_up[:, width:], 1, 1)
        ).astype(bf16)
        terms = dot(activated, down[...], 1, 0).astype(bf16)
        for part, spot in enumerate(spots):
            layer_terms[spot, :] = terms[part * size : (part + 1) * size]
            activated_out[spot, :] = activated[part * size : (part + 1) * size]
        return carry

    for side in range(2):
        lax.fori_loop(0, count, functools.partial(step, side), 0)


def mix_kernel(attended, spread, first, last, rows, gain, placed_out, mixed_out, normed_out):
    placed = dot(attended[...], spread[...], 1, 0).astype(bf16)
    placed_out[...] = placed
    mixed = rows[...].astype(f32) + times(placed, first, last, slice(0, WIDTH))
    mixed_out[...] = mixed
    unused, unit = rms(mixed)
    normed_out[...] = (unit * gain[...]).astype(bf16)


def rms_backward(residual, normed_grad, inverse, unit, gain):
    scaled = normed_grad * gain
    return residual + inverse * (scaled - unit * jnp.mean(scaled * unit, -1, keepdims=True))


def unmix_kernel(
    normed_grad, mixed, cotangent, gain, spread, first, last,
    mixed_grad_out, mixed_low_out, attended_grad, gain_grad,
):
    inverse, unit = rms(mixed[...])
    grad = normed_grad[...].astype(f32)
    gain_grad[...] = jnp.sum(grad * unit, 0, keepdims=True)
    mixed_grad = rms_backward(cotangent[...].astype(f32), grad, inverse, unit, gain[...])
    mixed_grad_out[...] = mixed_grad
    mixed_low = mixed_grad.astype(bf16)
    mixed_low_out[...] = mixed_low
    placed = times_over(mixed_low, first, last, slice(0, WIDTH)).astype(bf16)
    attended_grad[...] = dot(placed, spread[...], 1, 1).astype(bf16)


def finish_kernel(
    sizes, query_grad, key_grad, cosine, sine, rows, gain, spread, marks, owner, first, last,
    placed_normed, mixed_grad, mlp_gain_grad,
    input_grad, part_first, part_last,
):
    cos, sin = cosine[...], sine[...]
    dquery = turn(query_grad[...], cos, sin, -1.0)
    dkey = turn(key_grad[:, :KEY_WIDTH], cos, sin, -1.0)
    dvalue = key_grad[:, KEY_WIDTH:]
    low = jnp.concatenate([dquery, dkey, dvalue], 1).astype(bf16)
    normed_grad = split_dot(
        times_over(low, first, last, slice(0, WIDTH + 2 * KEY_WIDTH)), spread[...], 1, 1
    )
    inverse, unit = rms(rows[...].astype(f32))
    input_grad[...] = rms_backward(mixed_grad[...], normed_grad, inverse, unit, gain[...])
    vectors = (
        jnp.sum(normed_grad * unit, 0, keepdims=True),
        jnp.sum(dquery, 0, keepdims=True),
        jnp.sum(dvalue, 0, keepdims=True),
        mlp_gain_grad[...],
    )
    spare, offset = jnp.zeros((owner.shape[0], LANES), f32), 0
    for (length, width), vector in zip(sizes, vectors):
        mine = jnp.where(owned_by(owner[...], width, length), vector, 0.0)
        spare = spare + split_dot(mine, lane_of(width, length, offset, LANES), 1, 0)
        offset = offset + length
    half = first.shape[0]
    over = placed_normed[...].astype(f32).T.astype(bf16)
    for at, out in ((0, part_first), (half, part_last)):
        part = dot(over[at : at + half], low, 1, 0)
        out[:, :LANES] = (
            part[:, :LANES] + dot(marks[at : at + half, :], spare.astype(bf16), 1, 0)
        ).astype(bf16)
        out[:, LANES:] = part[:, LANES:].astype(bf16)


def update_kernel(hidden, sums, *refs):
    plane, rows, width = sums.shape
    half = width // 2
    depth = refs[0].shape[1] // (plane * hidden)
    for at in range(2):
        weight, first, second = refs[3 * at : 3 * at + 3]
        gradient, weight_new, first_new, second_new = refs[6 + 4 * at : 10 + 4 * at]
        for z in range(depth):
            for t in range(plane):
                start = (z * plane + t) * hidden
                source = at * half + z * hidden
                gradient[:, start : start + hidden] = sums[t, :, source : source + hidden].astype(f32)
        weight_new[...], first_new[...], second_new[...] = adamw_update(
            weight[...], gradient[...], first[...], second[...], matrix_rate, decay_rate
        )


def call(kernel, outs, scratch=(), scalars=0, name=None, cost=1):
    return pl.pallas_call(
        kernel,
        out_shape=[jax.ShapeDtypeStruct(shape, kind) for shape, kind in outs],
        in_specs=None if scalars is None else scalars,
        out_specs=[VMEM] * len(outs),
        scratch_shapes=list(scratch),
        compiler_params=pltpu.CompilerParams(vmem_limit_bytes=56 * 1024 * 1024),
        cost_estimate=pl.CostEstimate(
            flops=cost * 1_000_000_000, bytes_accessed=cost * 3_000_000, transcendentals=0
        ),
        name=name,
    )


def per_device(plan, mesh_sources, token_sources_of, key_masks, *arguments):
    layer_input, positions, out_grad = arguments[:3]
    masters, first_moments, second_moments = arguments[3:13], arguments[13:23], arguments[23:33]
    (
        norm_gain, query_proj, query_bias, keyval_proj, value_bias,
        output_proj, mlp_gain, gate_proj, up_proj, down_proj,
    ) = masters
    depth, plane, total = plan.depth, plan.plane, plan.total
    own = lax.axis_index(AXES)
    token_rows, position_rows, cotangent = layer_input[0], positions[0], out_grad[0]
    token_count = token_rows.shape[0]
    size = token_count // 2
    rows = query_proj.shape[0]
    vectors = (norm_gain, query_bias, value_bias, mlp_gain)
    vector_sizes = [vector.shape[0] for vector in vectors]
    vector_total = sum(vector_sizes)
    padded = -(-(rows + 1) // 16) * 16
    half = padded // 2
    qkv_width = query_proj.shape[1] + keyval_proj.shape[1]
    sources = mesh_sources(padded)
    flat_sources = sources.reshape(-1, 2)
    order = sources.shape[:-2]
    vector_masks = flat_sources[flat_sources[:, 1] == rows, 0]

    (block,) = call(
        functools.partial(pack_kernel, size),
        [((padded, qkv_width + WIDTH), bf16)],
        scalars=[SMEM] + [VMEM] * 7,
        name="pack",
        cost=2,
    )(positions, query_proj, keyval_proj, output_proj, *[vector[None] for vector in vectors])
    gate_shard, up_shard, block = together(gate_proj, up_proj, block)
    deep_blocks = gather_deep(plan, block)
    owner = own ^ jnp.asarray(flat_sources[:, 0])
    target = jnp.where(
        jnp.asarray(flat_sources[:, 1] < rows), owner * rows + jnp.asarray(flat_sources[:, 1]), -1
    )
    count = target.shape[0]
    column = lax.broadcasted_iota(jnp.int32, (WIDTH, count), 0)
    spread = (column == target[None]).astype(bf16)
    place_own = own % plane

    exponents = jnp.arange(HEAD_DIM // 2, dtype=f32) * (-2.0 / HEAD_DIM)
    inverse_freq = jnp.tile(jnp.power(f32(rope_base), exponents), 4)
    angles = position_rows.astype(f32)[:, None] * inverse_freq[None, :]
    cosine, sine = jnp.cos(angles), jnp.sin(angles)

    hidden = down_proj.shape[0]
    slice_width = hidden * depth
    slice_padded = -(-slice_width // 128) * 128

    (gate_up_parts,) = call(
        functools.partial(slice_kernel, hidden),
        [((plane, rows, 2 * slice_padded), bf16)],
        scalars=[VMEM] * 2,
        name="slices",
        cost=2,
    )(gate_shard, up_shard)
    gate_up_rows = lax.all_to_all(gate_up_parts, ("t", "f"), split_axis=0, concat_axis=0, tiled=True)
    down_low = lax.all_gather(down_proj.astype(bf16), "z", axis=0, tiled=True)
    deep_blocks, gate_up_rows, spread, cosine, sine = together(
        deep_blocks, gate_up_rows, spread, cosine, sine
    )
    gate_up_low = lax.all_gather(
        gate_up_rows.reshape(plane * rows, 2 * slice_padded), "z", axis=0, tiled=True
    )
    weights = [
        blocks.reshape(-1, qkv_width)
        for blocks in gather_flat(plan, deep_blocks[:, :, :qkv_width])
    ]
    vector_owner = (own ^ jnp.asarray(vector_masks))[:, None]
    vector_at = flat_sources[:, 1] == rows
    marks = jnp.asarray(
        (np.flatnonzero(vector_at)[None] == np.arange(len(vector_at))[:, None]).astype(np.float32)
    ).astype(bf16)
    pairs = jnp.asarray((key_masks[:, None] == vector_masks[None]).astype(np.float32)).astype(bf16)
    sizes = [(length, length * total) for length in vector_sizes]

    placed_normed, query_rot, key_rot, value_low, gain_row, mlp_gain_row, place = call(
        functools.partial(project_kernel, sizes),
        [
            ((token_count, count), bf16),
            ((token_count, WIDTH), bf16),
            ((token_count, KEY_WIDTH), bf16),
            ((token_count, KEY_WIDTH), bf16),
            ((1, WIDTH), f32),
            ((1, WIDTH), f32),
            ((1, -(-2 * plan.ctx // LANES) * LANES), jnp.int32),
        ],
        scalars=[VMEM] * 9,
        name="project",
    )(token_rows, spread, marks, vector_owner, pairs, *weights, cosine, sine)

    output_blocks, key_rot = together(deep_blocks[:, :, qkv_width:], key_rot)
    deep_keys = gather_deep(plan, jnp.concatenate([key_rot, value_low], 1))
    output_weights = [blocks.reshape(-1, WIDTH) for blocks in gather_flat(plan, output_blocks)]
    all_keys = gather_keys(plan, deep_keys)
    cotangent, all_keys, output_weights = together(cotangent, all_keys, output_weights)
    all_cotangent = spread_flat(plan, cotangent).reshape(-1, WIDTH)
    key_rows = all_keys.shape[0] * token_count
    all_keys = all_keys.reshape(-1, 2 * KEY_WIDTH)
    chunk = KEY_CHUNK
    attended, log_total = call(
        functools.partial(attend_kernel, size, chunk),
        [((token_count, WIDTH), bf16), ((2 * KV_HEADS, GROUP * size), f32)],
        scratch=[
            pltpu.VMEM((key_rows, KEY_WIDTH), bf16),
            pltpu.VMEM((key_rows, KEY_WIDTH), bf16),
            pltpu.VMEM((KEY_WIDTH, key_rows), bf16),
        ],
        scalars=[SMEM, SMEM] + [VMEM] * 2,
        name="attend",
    )(place, positions, query_rot, all_keys)

    attended, gate_up_low = together(attended, gate_up_low)
    placed_attended, mixed, normed_mixed = call(
        mix_kernel,
        [
            ((token_count, count), bf16),
            ((token_count, WIDTH), f32),
            ((token_count, WIDTH), bf16),
        ],
        scalars=[VMEM] * 6,
        name="mix",
    )(attended, spread, *output_weights, token_rows, mlp_gain_row)

    normed_mixed, all_cotangent = together(normed_mixed, all_cotangent)
    normed_blocks, down_low = gather_flat(plan, normed_mixed[None], wait=down_low)
    token_order = normed_blocks[0].shape
    normed_blocks = [blocks.reshape(-1, WIDTH) for blocks in normed_blocks]
    token_total = 2 * normed_blocks[0].shape[0]
    moves = jnp.asarray(token_sources_of)
    places = (place_own ^ moves[:, 0]) * 2 + moves[:, 1]
    kept_terms, sent_terms, layer_terms, activated, hidden_grad = call(
        functools.partial(feed_kernel, size, 8),
        [
            ((token_total // 2, WIDTH), bf16),
            ((token_total // 2, WIDTH), bf16),
            ((token_total, WIDTH), bf16),
            ((token_total, slice_padded), bf16),
            ((token_total, 2 * slice_padded), bf16),
        ],
        scratch=[pltpu.VMEM((slice_padded, WIDTH), bf16)],
        scalars=[SMEM] + [VMEM] * 5,
        name="feed",
        cost=16,
    )(places, *normed_blocks, all_cotangent, gate_up_low, down_low)
    kept_terms = add_arrived(
        plan, kept_terms.reshape(token_order), sent_terms.reshape(token_order)
    )
    hidden_grad, kept_terms = together(hidden_grad, kept_terms)
    split = token_total // 2
    part_gate_up = (
        dot(normed_blocks[0], hidden_grad[:split], 0, 0)
        + dot(normed_blocks[1], hidden_grad[split:], 0, 0)
    ).astype(bf16)
    normed_mixed_grad = scatter_halves(plan, kept_terms)[0]
    layer_terms, normed_mixed_grad = together(layer_terms, normed_mixed_grad)

    mixed_grad, mixed_low, attended_grad, part_mgain = call(
        unmix_kernel,
        [
            ((token_count, WIDTH), f32),
            ((token_count, WIDTH), bf16),
            ((token_count, WIDTH), bf16),
            ((1, WIDTH), f32),
        ],
        scalars=[VMEM] * 7,
        name="unmix",
        cost=5,
    )(normed_mixed_grad, mixed, cotangent, mlp_gain_row, spread, *output_weights)

    gate_up_sum = lax.psum_scatter(part_gate_up, "z", scatter_dimension=0, tiled=True)
    layer_terms = layer_terms.reshape(plane, token_count, WIDTH)
    layer_terms = lax.all_to_all(layer_terms, ("t", "f"), split_axis=0, concat_axis=0, tiled=True)

    part_output = dot(placed_attended, mixed_low, 0, 0).astype(bf16)
    part_output = part_output.reshape(order + (half, WIDTH))
    part_output = add_arrived(plan, part_output[0], part_output[1])
    query_rot_grad, *key_terms = call(
        functools.partial(backward_kernel, size, chunk),
        [
            ((token_count, WIDTH), f32),
            ((key_rows // 2, 2 * KEY_WIDTH), bf16),
            ((key_rows // 2, 2 * KEY_WIDTH), bf16),
        ],
        scratch=[
            pltpu.VMEM((key_rows, KEY_WIDTH), bf16),
            pltpu.VMEM((key_rows, KEY_WIDTH), bf16),
            pltpu.VMEM((KEY_WIDTH, key_rows), bf16),
            pltpu.VMEM((KV_HEADS, key_rows, HEAD_DIM), f32),
            pltpu.VMEM((KV_HEADS, key_rows, HEAD_DIM), f32),
        ],
        scalars=[SMEM, SMEM] + [VMEM] * 5,
        name="backward",
        cost=16,
    )(place, positions, query_rot, all_keys, attended, attended_grad, log_total)
    key_terms, layer_terms = together(key_terms, layer_terms)
    key_terms = add_arrived(plan, *key_terms)
    activated, key_terms = together(activated, key_terms)
    part_down = dot(activated, all_cotangent, 0, 0)[:slice_width].astype(bf16)
    part_down, gate_up_sum = together(part_down, gate_up_sum)
    down_sum = lax.psum_scatter(part_down, "z", scatter_dimension=0, tiled=True)
    key_sum = scatter_keys(plan, key_terms)

    gate_up_sum = lax.all_to_all(
        gate_up_sum.reshape(plane, rows, 2 * slice_padded),
        ("t", "f"), split_axis=0, concat_axis=0, tiled=True,
    )
    layer_rows = (mixed + jnp.sum(layer_terms.astype(f32), 0)).astype(bf16)
    input_rows, *part_qkv = call(
        functools.partial(finish_kernel, sizes),
        [
            ((token_count, WIDTH), f32),
            ((count // 2, qkv_width), bf16),
            ((count // 2, qkv_width), bf16),
        ],
        scalars=[VMEM] * 14,
        name="finish",
        cost=9,
    )(
        query_rot_grad, key_sum, cosine, sine, token_rows, gain_row, spread, marks, vector_owner,
        *weights, placed_normed, mixed_grad, part_mgain,
    )
    part_qkv = [part.reshape(order[1:] + (half, qkv_width)) for part in part_qkv]
    part_qkv, gate_up_sum = together(part_qkv, gate_up_sum)
    part_qkv = add_arrived(plan, *part_qkv)
    gate_up_sum, part_qkv = together(gate_up_sum, part_qkv)
    gate_up_news = call(
        functools.partial(update_kernel, hidden),
        [(gate_proj.shape, f32)] * 8,
        scalars=[VMEM] * 7,
        name="update",
        cost=6,
    )(
        gate_up_sum, gate_proj, first_moments[7], second_moments[7],
        up_proj, first_moments[8], second_moments[8],
    )
    weight_sums, gate_up_news = scatter_halves(
        plan, jnp.concatenate([part_qkv, part_output], -1), gate_up_news
    )
    grad_gate, *new_gate, grad_up, new_up, new_up_mean, new_up_square = gate_up_news
    weight_sums = scatter_deep(plan, weight_sums)
    qkv_sum = weight_sums[:, :qkv_width]
    grad_output = weight_sums[:rows, qkv_width:]

    new_up = [new_up, new_up_mean, new_up_square]
    grad_down = down_sum.astype(f32)
    grad_query = qkv_sum[:rows, :WIDTH]
    grad_keyval = qkv_sum[:rows, WIDTH:]
    vector_sums = qkv_sum[rows]
    vector_grads = []
    offset = 0
    for length in vector_sizes:
        vector_grads.append(vector_sums[offset : offset + length])
        offset = offset + length
    grad_gain, grad_qbias, grad_vbias, grad_mgain = vector_grads
    gradients = (
        grad_gain, grad_query, grad_qbias, grad_keyval, grad_vbias,
        grad_output, grad_mgain, grad_gate, grad_up, grad_down,
    )
    vector, matrix = (vector_rate, 0.0), (matrix_rate, decay_rate)
    settings = (
        vector, matrix, vector, matrix, vector, (output_rate, decay_rate), vector,
        matrix, matrix, matrix,
    )
    updated = [
        adamw_update(weight, gradient, first_moment, second, setting[0], setting[1])
        for weight, gradient, first_moment, second, setting in zip(
            masters, gradients, first_moments, second_moments, settings
        )
    ]
    updated[7], updated[8] = new_gate, new_up
    return (
        (layer_rows[None], input_rows[None])
        + tuple(gradients)
        + tuple((entry[0] for entry in updated))
        + tuple((entry[1] for entry in updated))
        + tuple((entry[2] for entry in updated))
    )


def solution(mesh):
    plan = Plan(mesh)
    devices = mesh.devices.reshape(plan.depth, plan.across, plan.seqs)
    return jax.shard_map(
        functools.partial(
            per_device, plan, functools.partial(row_sources, mesh), token_sources(mesh),
            key_sources(mesh),
        ),
        mesh=Mesh(devices, AXES),
        in_specs=(
            P("f", ("z", "t"), None),
            P("f", ("z", "t")),
            P("f", ("z", "t"), None),
            P(AXES),
            P(AXES, None),
            P(AXES),
            P(AXES, None),
            P(AXES),
            P(AXES, None),
            P(AXES),
            P(AXES, None),
            P(AXES, None),
            P(AXES, None),
            P(AXES),
            P(AXES, None),
            P(AXES),
            P(AXES, None),
            P(AXES),
            P(AXES, None),
            P(AXES),
            P(AXES, None),
            P(AXES, None),
            P(AXES, None),
            P(AXES),
            P(AXES, None),
            P(AXES),
            P(AXES, None),
            P(AXES),
            P(AXES, None),
            P(AXES),
            P(AXES, None),
            P(AXES, None),
            P(AXES, None),
        ),
        out_specs=(
            P("f", ("z", "t"), None),
            P("f", ("z", "t"), None),
            P(AXES),
            P(AXES, None),
            P(AXES),
            P(AXES, None),
            P(AXES),
            P(AXES, None),
            P(AXES),
            P(AXES, None),
            P(AXES, None),
            P(AXES, None),
            P(AXES),
            P(AXES, None),
            P(AXES),
            P(AXES, None),
            P(AXES),
            P(AXES, None),
            P(AXES),
            P(AXES, None),
            P(AXES, None),
            P(AXES, None),
            P(AXES),
            P(AXES, None),
            P(AXES),
            P(AXES, None),
            P(AXES),
            P(AXES, None),
            P(AXES),
            P(AXES, None),
            P(AXES, None),
            P(AXES, None),
            P(AXES),
            P(AXES, None),
            P(AXES),
            P(AXES, None),
            P(AXES),
            P(AXES, None),
            P(AXES),
            P(AXES, None),
            P(AXES, None),
            P(AXES, None),
        ),
        check_vma=False,
    )
```
